512 devices in a mesh: inter: 16 (over x, y_lo, core), intra: 32 (over y_hi, z).
Axes of the slice: x: 4, y: 8 (y_hi: 4, y_lo: 2; y = y_hi * 2 + y_lo), z: 8, core: 2. Of those that a mesh axis runs over, the one named last changes fastest.
Arguments:
- acts: bfloat16 [65536, 256], P(('inter', 'intra')), may hold values from -4 to 4, as said below
- cotangent: bfloat16 [65536, 14336], P(('inter', 'intra')), may hold values from -2 to 2, as said below
- first_exp: int32 [256, 112], replicated, may hold values from 0 to 3
- second_exp: int32 [256, 112], P('intra'), may hold values from 4 to 6
Outputs:
- grad_shard: float32 [256, 14336], P('intra', 'inter')
The draws below stay inside these ranges and needn't reach their ends.
Inputs may be any that keep to these rules, and one draw needn't show every extreme that they name: `acts`: entries are multiples of 1/32. `cotangent`: entries are multiples of 1/64.
All inputs are finite; a program needn't handle non-finite values.
Results may differ from the reference program's by a relative error of at most 0.0003.
Values may be sent and summed in bfloat16 or wider, within the bound.
No kernel may reach another device: no remote copies, remote signals or barrier semaphores. Data moves between devices by JAX's collectives and lax.ppermute only.
A program may use at most 64 MiB of HBM per device.

```python
import jax
import jax.numpy as jnp
from jax import lax

FF = 14336
ROWS = 256
TOK_DEV = 128
BLK = 128
NBLK = 112
TOKENS = 65536
N_INTER = 16
N_INTRA = 32


def draw_acts(key, part):
    key = jax.random.fold_in(key, 11)
    values = jax.random.randint(key, (TOKENS, ROWS), -64, 65)
    return (values.astype(jnp.float32) / 16.0).astype(jnp.bfloat16)


def draw_cotangent(key, part):
    key = jax.random.fold_in(key, 12)
    values = jax.random.randint(key, (TOKENS, FF), -96, 97)
    return (values.astype(jnp.float32) / 64.0).astype(jnp.bfloat16)


def set_ends(entries, key, low, high):
    place = [jax.random.randint(jax.random.fold_in(key, axis), (), 0, length) for axis, length in enumerate(entries.shape)]
    longest = entries.shape.index(max(entries.shape))
    next_to = place[:longest] + [(place[longest] + 1) % entries.shape[longest]] + place[longest + 1:]
    return entries.at[tuple(place)].set(low).at[tuple(next_to)].set(high)


def setup_inputs(seed: int = 0) -> dict:
    key_of = jax.random.split(jax.random.key(seed), 5)
    return {
        "acts": draw_acts(jax.random.fold_in(key_of[4], 71), 0),
        "cotangent": draw_cotangent(jax.random.fold_in(key_of[4], 71), 0),
        "first_exp": set_ends(jax.random.randint(key_of[2], (ROWS, NBLK), 0, 4), jax.random.fold_in(key_of[2], 1), 0, 3).astype(jnp.int32),
        "second_exp": set_ends(jax.random.randint(key_of[3], (ROWS, NBLK), 4, 7), jax.random.fold_in(key_of[3], 1), 4, 6).astype(jnp.int32),
    }


def power_two(expo):
    total = jnp.zeros(expo.shape, jnp.float32)
    for power in range(-8, 9):
        total = total + jnp.where(expo == power, jnp.float32(2.0 ** power), jnp.float32(0.0))
    return total


def round_even(values):
    lower = jnp.floor(values)
    part = values - lower
    parity = lower - 2.0 * jnp.floor(lower * 0.5)
    return jnp.where(part > 0.5, lower + 1.0, jnp.where(part < 0.5, lower, lower + parity))


def apply_scale(values, scale):
    row_count, col_count = values.shape
    shaped = values.reshape(row_count, col_count // BLK, BLK) * scale[:, :, None]
    return shaped.reshape(row_count, col_count)


def quantize(values, inverse):
    return round_even(jnp.clip(apply_scale(values, inverse), -127.0, 127.0))


def reference(acts, cotangent, first_exp, second_exp):
    scale_one = power_two(first_exp)
    inverse_one = power_two(-first_exp)
    scale_two = power_two(second_exp)
    inverse_two = power_two(-second_exp)
    group_acts = acts.reshape(N_INTER, N_INTRA, TOK_DEV, ROWS)
    group_cot = cotangent.reshape(N_INTER, N_INTRA, TOK_DEV, FF)

    def member_step(total, pair):
        act_block, cot_block = pair
        local = lax.dot_general(act_block, cot_block, (((0,), (0,)), ((), ())), preferred_element_type=jnp.float32)
        codes = quantize(local, inverse_one).astype(jnp.bfloat16)
        return total + codes.astype(jnp.float32), None

    def group_step(total, pair):
        code_sum, unused = lax.scan(member_step, jnp.zeros((ROWS, FF), jnp.float32), pair)
        summed = apply_scale(code_sum, scale_one)
        second = quantize(summed, inverse_two).astype(jnp.bfloat16)
        return total + second.astype(jnp.float32), None

    total, unused = lax.scan(group_step, jnp.zeros((ROWS, FF), jnp.float32), (group_acts, group_cot))
    return apply_scale(total, scale_two) * (1.0 / (N_INTER * N_INTRA))
```

```python
import jax
import jax.numpy as jnp
from jax import lax
from jax.experimental import pallas as pl
from jax.experimental.pallas import tpu as pltpu
from jax.sharding import PartitionSpec as P

BLK = 128
NY = 4
NZ = 8
NG = 16
NM = NY * NZ
HALF = 7168
CZ = HALF // NZ
CY = HALF // NY
OFFS = (2, 1, -1)
MAGIC = 12582912.0
Z_GROUPS = [[y * NZ + z for z in range(NZ)] for y in range(NY)]
Y_GROUPS = [[y * NZ + z for y in range(NY)] for z in range(NZ)]


def y_shift(step):
    return [(y * NZ + z, ((y + step) % NY) * NZ + z) for y in range(NY) for z in range(NZ)]


def last_moves(flip):
    moves = []
    for group in range(NG):
        k, h = group // 2, group % 2
        for y in range(NY):
            for z in range(NZ):
                if h == flip:
                    target = z * NM + y * NZ + k
                else:
                    target = (8 + 2 * y + k % 2) * NM + (k // 2) * NZ + z
                moves.append((group * NM + y * NZ + z, target))
    return moves


def power_two(expo):
    total = jnp.zeros(expo.shape, jnp.float32)
    for power in range(-8, 9):
        total = total + jnp.where(expo == power, jnp.float32(2.0**power), jnp.float32(0.0))
    return total


def round_clip(values):
    return (jnp.clip(values, -127.0, 127.0) + MAGIC) - MAGIC


def pack_kernel(pos, acts, cot, hz, p2, p1, p3, sems):
    y = pos[0]
    copies = []
    for j in range(NZ):
        copies.append((cot.at[:, j * CZ : (j + 1) * CZ], hz.at[j]))
    for step, out in zip(OFFS, (p2, p1, p3)):
        start = HALF + CY * lax.rem(y + step + NY, NY)
        copies.append((cot.at[:, pl.ds(pl.multiple_of(start, CY), CY)], out.at[:, 0:CY]))
        copies.append((acts, out.at[:, CY : CY + 256]))
    started = [pltpu.make_async_copy(src, dst, sems.at[i]) for i, (src, dst) in enumerate(copies)]
    for copy in started:
        copy.start()
    for copy in started:
        copy.wait()


def pack(pos, acts, cot):
    any_spec = pl.BlockSpec(memory_space=pl.ANY)
    wide = jax.ShapeDtypeStruct((128, CY + 256), jnp.bfloat16)
    return pl.pallas_call(
        pack_kernel,
        out_shape=[jax.ShapeDtypeStruct((NZ, 128, CZ), jnp.bfloat16), wide, wide, wide],
        in_specs=[pl.BlockSpec(memory_space=pltpu.SMEM), any_spec, any_spec],
        out_specs=[any_spec] * 4,
        scratch_shapes=[pltpu.SemaphoreType.DMA((NZ + 6,))],
        cost_estimate=pl.CostEstimate(flops=0, bytes_accessed=7000000, transcendentals=0),
    )(pos, acts, cot)


def spread(inverse, first_block, width):
    block = lax.broadcasted_iota(jnp.int32, (BLK, width), 0)
    column = lax.broadcasted_iota(jnp.int32, (BLK, width), 1)
    pick = jnp.where(block == first_block + column // BLK, 1.0, 0.0).astype(jnp.bfloat16)
    return jnp.dot(inverse, pick, preferred_element_type=jnp.float32)


def sum_y_kernel(pos, lhs, inverse, own, q2, q1, q3, out):
    i = pl.program_id(0)
    scale = spread(inverse[...], HALF // BLK + pos[0] * (CY // BLK) + 2 * i, 256)
    total = jnp.zeros((256, 256), jnp.float32)
    for r, part in enumerate((own, q2, q1, q3)):
        local = jnp.dot(lhs[r], part[...], preferred_element_type=jnp.float32)
        total = total + round_clip(local * scale)
    for z in range(NZ):
        rows = [total[64 * y + 8 * z : 64 * y + 8 * z + 8] for y in range(NY)]
        out[z] = jnp.concatenate(rows, axis=0).astype(jnp.int16)


def sum_y(pos, lhs, inverse, cot, q2, q1, q3):
    def piece(i, pos):
        return (0, i)

    return pl.pallas_call(
        sum_y_kernel,
        out_shape=jax.ShapeDtypeStruct((NZ, 32, CY), jnp.int16),
        grid_spec=pltpu.PrefetchScalarGridSpec(
            num_scalar_prefetch=1,
            grid=(CY // 256,),
            in_specs=[
                pl.BlockSpec((4, 256, 128), lambda i, pos: (0, 0, 0)),
                pl.BlockSpec((256, BLK), lambda i, pos: (0, 0)),
                pl.BlockSpec((128, 256), lambda i, pos: (0, HALF // 256 + pos[0] * (CY // 256) + i)),
                pl.BlockSpec((128, 256), piece),
                pl.BlockSpec((128, 256), piece),
                pl.BlockSpec((128, 256), piece),
            ],
            out_specs=pl.BlockSpec((NZ, 32, 256), lambda i, pos: (0, 0, i)),
        ),
        cost_estimate=pl.CostEstimate(flops=2 * 4 * 256 * 128 * CY, bytes_accessed=3000000, transcendentals=0),
    )(pos, lhs, inverse, cot, q2, q1, q3)


def sum_z_kernel(pos, lhs, inverse, parts, own, s2, s1, s3, total_ref):
    i = pl.program_id(0)
    y = pos[0]
    scale = spread(inverse[...], pos[1] * (CZ // BLK) + i, BLK)
    total = jnp.zeros((256, BLK), jnp.float32)
    for r in range(NZ):
        local = jnp.dot(lhs[r], parts[r], preferred_element_type=jnp.float32)
        total = total + round_clip(local * scale)
    total_ref[...] = total
    for step, out in zip((0,) + OFFS, (own, s2, s1, s3)):
        start = 64 * lax.rem(y + step + NY, NY)
        out[...] = total_ref[pl.ds(pl.multiple_of(start, 64), 64), :].astype(jnp.int16)


def sum_z(pos, lhs, inverse, parts):
    return pl.pallas_call(
        sum_z_kernel,
        out_shape=[jax.ShapeDtypeStruct((64, CZ), jnp.int16)] * 4,
        grid_spec=pltpu.PrefetchScalarGridSpec(
            num_scalar_prefetch=1,
            grid=(CZ // BLK,),
            in_specs=[
                pl.BlockSpec((NZ, 256, 128), lambda i, pos: (0, 0, 0)),
                pl.BlockSpec((256, BLK), lambda i, pos: (0, 0)),
                pl.BlockSpec((NZ, 128, BLK), lambda i, pos: (0, 0, i)),
            ],
            out_specs=[pl.BlockSpec((64, BLK), lambda i, pos: (0, i))] * 4,
            scratch_shapes=[pltpu.VMEM((256, BLK), jnp.float32)],
        ),
        cost_estimate=pl.CostEstimate(flops=2 * 8 * 256 * 128 * CZ, bytes_accessed=3000000, transcendentals=0),
    )(pos, lhs, inverse, parts)


def second_kernel(own, s2, s1, s3, sy, scale_z, scale_y, out):
    total = own[...].astype(jnp.float32)
    for part in (s2, s1, s3):
        total = total + part[...].astype(jnp.float32)
    qz = round_clip(total * scale_z[...])
    total = sy[0].astype(jnp.float32)
    for r in range(1, NZ):
        total = total + sy[r].astype(jnp.float32)
    qy = round_clip(total * scale_y[...])
    for k in range(8):
        zk = qz[8 * k : 8 * k + 8]
        yk = qy[8 * (k // 2) : 8 * (k // 2) + 8, CZ * (k % 2) : CZ * (k % 2) + CZ]
        out[2 * k] = jnp.concatenate([zk[0:4], yk[0:4]], axis=0).astype(jnp.bfloat16)
        out[2 * k + 1] = jnp.concatenate([zk[4:8], yk[4:8]], axis=0).astype(jnp.bfloat16)


def second_codes(own, s2, s1, s3, sy, scale_z, scale_y):
    return pl.pallas_call(
        second_kernel,
        out_shape=jax.ShapeDtypeStruct((NG, 8, CZ), jnp.bfloat16),
        cost_estimate=pl.CostEstimate(flops=4000000, bytes_accessed=2500000, transcendentals=0),
    )(own, s2, s1, s3, sy, scale_z, scale_y)


def body(acts, cotangent, first_exp, second_exp):
    member = lax.axis_index("intra")
    group = lax.axis_index("inter")
    y, z = member // NZ, member % NZ
    pos = jnp.stack([y, z]).astype(jnp.int32)

    hz, p2, p1, p3 = pack(pos, acts, cotangent)
    rz = lax.all_to_all(hz, "intra", 0, 0, axis_index_groups=Z_GROUPS, tiled=True)
    q2, q1, q3 = [lax.ppermute(p, "intra", y_shift(step)) for step, p in zip(OFFS, (p2, p1, p3))]

    inverse = jnp.pad(power_two(-first_exp), ((0, 0), (0, BLK - first_exp.shape[1]))).astype(jnp.bfloat16)
    extra = jnp.pad(second_exp, ((0, 0), (0, 256 - second_exp.shape[1]))).astype(jnp.bfloat16)
    along_z = lax.all_gather(jnp.concatenate([acts, extra], 0), "intra", axis_index_groups=Z_GROUPS)
    exp_y = lax.all_gather(second_exp, "intra", axis_index_groups=Y_GROUPS)
    lhs_z = jnp.swapaxes(along_z[:, :128], 1, 2)
    lhs_y = jnp.swapaxes(jnp.stack([acts] + [q[:, CY:] for q in (q2, q1, q3)]), 1, 2)

    blocks_z, blocks_y = CZ // BLK, CY // BLK
    second_z = along_z[:, 128:, : first_exp.shape[1]].reshape(64, -1).astype(jnp.int32)
    first_z = lax.dynamic_slice_in_dim(first_exp, 64 * y, 64, 0)
    diff_z = lax.dynamic_slice_in_dim(first_z - second_z, blocks_z * z, blocks_z, 1)
    scale_z = jnp.repeat(power_two(diff_z), BLK, axis=1)
    first_y = lax.dynamic_slice_in_dim(first_exp.reshape(NY, NZ, 8, -1), z, 1, 1).reshape(32, -1)
    diff_y = first_y - exp_y.reshape(32, -1)
    diff_y = lax.dynamic_slice_in_dim(diff_y, HALF // BLK + blocks_y * y, blocks_y, 1)
    scale_y = jnp.repeat(power_two(diff_y), BLK, axis=1)

    sy = sum_y(pos, lhs_y, inverse, cotangent, q2, q1, q3)
    ry = lax.all_to_all(sy, "intra", 0, 0, axis_index_groups=Z_GROUPS, tiled=True)
    own, s2, s1, s3 = sum_z(pos, lhs_z, inverse, rz)
    t2, t1, t3 = [lax.ppermute(s, "intra", y_shift(step)) for step, s in zip(OFFS, (s2, s1, s3))]
    second = second_codes(own, t2, t1, t3, ry, scale_z, scale_y)

    received = lax.all_to_all(second, "inter", 0, 0, tiled=True)
    total = jnp.sum(received, axis=0, dtype=jnp.float32)
    part_z, part_y = total[:4], total[4:]
    low = group % 2 == 0
    one = lax.ppermute(jnp.where(low, part_z, part_y), ("inter", "intra"), last_moves(0))
    two = lax.ppermute(jnp.where(low, part_y, part_z), ("inter", "intra"), last_moves(1))
    rows = jnp.where(group < 8, jnp.concatenate([one, two], 0), jnp.concatenate([two, one], 0))
    my_exp = lax.dynamic_slice_in_dim(second_exp, group * blocks_z, blocks_z, 1)
    return rows * (jnp.repeat(power_two(my_exp), BLK, axis=1) * (1.0 / (NG * NM)))


def solution(mesh):
    return jax.shard_map(
        body,
        mesh=mesh,
        in_specs=(P(("inter", "intra"), None), P(("inter", "intra"), None), P(), P("intra", None)),
        out_specs=P("intra", "inter"),
        check_vma=False,
    )
```

```python
import jax
import jax.numpy as jnp
from jax import lax
from jax.experimental import pallas as pl
from jax.experimental.pallas import tpu as pltpu
from jax.sharding import PartitionSpec as P

BLK = 128
NY = 4
NZ = 8
NG = 16
NM = NY * NZ
HALF = 7168
CZ = HALF // NZ
CY = HALF // NY
OFFS = (2, 1, -1)
MAGIC = 12582912.0
Z_GROUPS = [[y * NZ + z for z in range(NZ)] for y in range(NY)]


def y_shift(step):
    return [(y * NZ + z, ((y + step) % NY) * NZ + z) for y in range(NY) for z in range(NZ)]


def last_moves():
    moves = []
    for group in range(NG):
        for y in range(NY):
            for z in range(NZ):
                if group < 8:
                    target = z * NM + y * NZ + group
                else:
                    target = (8 + 2 * y + group % 2) * NM + ((group - 8) // 2) * NZ + z
                moves.append((group * NM + y * NZ + z, target))
    return moves


def power_two(expo):
    total = jnp.zeros(expo.shape, jnp.float32)
    for power in range(-8, 9):
        total = total + jnp.where(expo == power, jnp.float32(2.0**power), jnp.float32(0.0))
    return total


def round_clip(values):
    return (jnp.clip(values, -127.0, 127.0) + MAGIC) - MAGIC


def pack_z_kernel(acts, exps, cot, out, held, padded, into, outof):
    loads = []
    for j in range(NZ):
        for b in range(CZ // BLK):
            column = j * CZ + b * BLK
            rows = pl.ds(256 + b * BLK, BLK)
            loads.append(
                pltpu.make_async_copy(cot.at[:, column : column + BLK], held.at[j, rows, :], into.at[len(loads)])
            )
    for load in loads:
        load.start()
    turned = acts[...].T
    padded[...] = jnp.zeros((16, BLK), jnp.float32)
    padded[0:8, 0 : exps.shape[1]] = exps[...].astype(jnp.float32)
    tail = padded[...].astype(jnp.bfloat16)
    for j in range(NZ):
        held[j, 0:256, :] = turned
        held[j, 256 + CZ : 256 + CZ + 16, :] = tail
    stores = [pltpu.make_async_copy(held.at[j], out.at[j], outof.at[j]) for j in range(NZ)]
    for j in range(NZ):
        for b in range(CZ // BLK):
            loads[j * (CZ // BLK) + b].wait()
        stores[j].start()
    for store in stores:
        store.wait()


def pack_z(acts, exps, cot):
    shape = (NZ, 256 + CZ + 16, BLK)
    any_spec = pl.BlockSpec(memory_space=pl.ANY)
    vmem_spec = pl.BlockSpec(memory_space=pltpu.VMEM)
    return pl.pallas_call(
        pack_z_kernel,
        out_shape=jax.ShapeDtypeStruct(shape, jnp.bfloat16),
        in_specs=[vmem_spec, vmem_spec, any_spec],
        out_specs=any_spec,
        scratch_shapes=[
            pltpu.VMEM(shape, jnp.bfloat16),
            pltpu.VMEM((16, BLK), jnp.float32),
            pltpu.SemaphoreType.DMA((HALF // BLK,)),
            pltpu.SemaphoreType.DMA((NZ,)),
        ],
        cost_estimate=pl.CostEstimate(flops=0, bytes_accessed=4000000, transcendentals=0),
    )(acts, exps, cot)


def pack_y_kernel(pos, hz, cot, p2, p1, p3, held, into, outof):
    loads, stores = [], []
    per = CY // BLK + 2
    for i, (step, out) in enumerate(zip(OFFS, (p2, p1, p3))):
        start = HALF + CY * lax.rem(pos[0] + step + NY, NY)
        moves = [(hz.at[0, 0:256], held.at[i, 0:256]), (hz.at[0, pl.ds(256 + CZ, 16)], held.at[i, pl.ds(256 + CY, 16)])]
        for b in range(CY // BLK):
            column = pl.multiple_of(start + b * BLK, BLK)
            moves.append((cot.at[:, pl.ds(column, BLK)], held.at[i, pl.ds(256 + b * BLK, BLK), :]))
        loads += [pltpu.make_async_copy(src, dst, into.at[i * per + k]) for k, (src, dst) in enumerate(moves)]
        stores.append(pltpu.make_async_copy(held.at[i], out, outof.at[i]))
    for load in loads:
        load.start()
    for i in range(3):
        for k in range(per):
            loads[i * per + k].wait()
        stores[i].start()
    for store in stores:
        store.wait()


def pack_y(pos, hz, cot):
    any_spec = pl.BlockSpec(memory_space=pl.ANY)
    piece = jax.ShapeDtypeStruct((256 + CY + 16, BLK), jnp.bfloat16)
    return pl.pallas_call(
        pack_y_kernel,
        out_shape=[piece, piece, piece],
        in_specs=[pl.BlockSpec(memory_space=pltpu.SMEM), any_spec, any_spec],
        out_specs=[any_spec] * 3,
        scratch_shapes=[
            pltpu.VMEM((3, 256 + CY + 16, BLK), jnp.bfloat16),
            pltpu.SemaphoreType.DMA((3 * (CY // BLK + 2),)),
            pltpu.SemaphoreType.DMA((3,)),
        ],
        cost_estimate=pl.CostEstimate(flops=0, bytes_accessed=3000000, transcendentals=0),
    )(pos, hz, cot)


def spread(inverse, first_block, width):
    block = lax.broadcasted_iota(jnp.int32, (BLK, width), 0)
    column = lax.broadcasted_iota(jnp.int32, (BLK, width), 1)
    pick = jnp.where(block == first_block + column // BLK, 1.0, 0.0).astype(jnp.bfloat16)
    return jnp.dot(inverse, pick, preferred_element_type=jnp.float32)


def sum_y_kernel(pos, inverse, own_lhs, lhs2, lhs1, lhs3, own, q2, q1, q3, out):
    i = pl.program_id(0)
    scale = spread(inverse[...], HALF // BLK + pos[0] * (CY // BLK) + 2 * i, 256)
    local = jnp.dot(own_lhs[0], own[...], preferred_element_type=jnp.float32)
    total = round_clip(local * scale)
    for lhs, part in ((lhs2, q2), (lhs1, q1), (lhs3, q3)):
        both = jnp.concatenate([part[0:BLK], part[BLK : 2 * BLK]], axis=1)
        local = jnp.dot(lhs[...], both, preferred_element_type=jnp.float32)
        total = total + round_clip(local * scale)
    for z in range(NZ):
        rows = [total[64 * y + 8 * z : 64 * y + 8 * z + 8] for y in range(NY)]
        out[z] = jnp.concatenate(rows, axis=0).astype(jnp.int16)


def sum_y(pos, inverse, hz, cot, q2, q1, q3):
    lhs = pl.BlockSpec((256, BLK), lambda i, pos: (0, 0))
    piece = pl.BlockSpec((256, BLK), lambda i, pos: (1 + i, 0))
    return pl.pallas_call(
        sum_y_kernel,
        out_shape=jax.ShapeDtypeStruct((NZ, 32, CY), jnp.int16),
        grid_spec=pltpu.PrefetchScalarGridSpec(
            num_scalar_prefetch=1,
            grid=(CY // 256,),
            in_specs=[
                pl.BlockSpec((256, BLK), lambda i, pos: (0, 0)),
                pl.BlockSpec((1, 256, BLK), lambda i, pos: (0, 0, 0)),
                lhs,
                lhs,
                lhs,
                pl.BlockSpec((128, 256), lambda i, pos: (0, HALF // 256 + pos[0] * (CY // 256) + i)),
                piece,
                piece,
                piece,
            ],
            out_specs=pl.BlockSpec((NZ, 32, 256), lambda i, pos: (0, 0, i)),
        ),
        cost_estimate=pl.CostEstimate(flops=2 * 4 * 256 * 128 * CY, bytes_accessed=3000000, transcendentals=0),
    )(pos, inverse, hz, q2, q1, q3, cot, q2, q1, q3)


def sum_z_kernel(pos, inverse, lhs, parts, own, s2, s1, s3, total_ref):
    i = pl.program_id(0)
    y = pos[0]
    scale = spread(inverse[...], pos[1] * (CZ // BLK) + i, BLK)
    total = jnp.zeros((256, BLK), jnp.float32)
    for r in range(NZ):
        local = jnp.dot(lhs[r], parts[r], preferred_element_type=jnp.float32)
        total = total + round_clip(local * scale)
    total_ref[...] = total
    for step, out in zip((0,) + OFFS, (own, s2, s1, s3)):
        start = 64 * lax.rem(y + step + NY, NY)
        out[...] = total_ref[pl.ds(pl.multiple_of(start, 64), 64), :].astype(jnp.int16)


def sum_z(pos, inverse, parts):
    return pl.pallas_call(
        sum_z_kernel,
        out_shape=[jax.ShapeDtypeStruct((64, CZ), jnp.int16)] * 4,
        grid_spec=pltpu.PrefetchScalarGridSpec(
            num_scalar_prefetch=1,
            grid=(CZ // BLK,),
            in_specs=[
                pl.BlockSpec((256, BLK), lambda i, pos: (0, 0)),
                pl.BlockSpec((NZ, 256, BLK), lambda i, pos: (0, 0, 0)),
                pl.BlockSpec((NZ, BLK, BLK), lambda i, pos: (0, 2 + i, 0)),
            ],
            out_specs=[pl.BlockSpec((64, BLK), lambda i, pos: (0, i))] * 4,
            scratch_shapes=[pltpu.VMEM((256, BLK), jnp.float32)],
        ),
        cost_estimate=pl.CostEstimate(flops=2 * 8 * 256 * 128 * CZ, bytes_accessed=3000000, transcendentals=0),
    )(pos, inverse, parts, parts)


def second_kernel(own, s2, s1, s3, sy, scale_z, scale_y, out):
    total = own[...].astype(jnp.float32)
    for part in (s2, s1, s3):
        total = total + part[...].astype(jnp.float32)
    qz = round_clip(total * scale_z[...])
    total = sy[0].astype(jnp.float32)
    for r in range(1, NZ):
        total = total + sy[r].astype(jnp.float32)
    qy = round_clip(total * scale_y[...])
    for k in range(8):
        out[k] = qz[8 * k : 8 * k + 8].astype(jnp.bfloat16)
        yk = qy[8 * (k // 2) : 8 * (k // 2) + 8, CZ * (k % 2) : CZ * (k % 2) + CZ]
        out[8 + k] = yk.astype(jnp.bfloat16)


def second_codes(own, s2, s1, s3, sy, scale_z, scale_y):
    return pl.pallas_call(
        second_kernel,
        out_shape=jax.ShapeDtypeStruct((NG, 8, CZ), jnp.bfloat16),
        cost_estimate=pl.CostEstimate(flops=4000000, bytes_accessed=2500000, transcendentals=0),
    )(own, s2, s1, s3, sy, scale_z, scale_y)


def body(acts, cotangent, first_exp, second_exp):
    member = lax.axis_index("intra")
    group = lax.axis_index("inter")
    y, z = member // NZ, member % NZ
    pos = jnp.stack([y, z]).astype(jnp.int32)

    hz = pack_z(acts, second_exp, cotangent)
    rz = lax.all_to_all(hz, "intra", 0, 0, axis_index_groups=Z_GROUPS, tiled=True)
    q2, q1, q3 = [lax.ppermute(p, "intra", y_shift(step)) for step, p in zip(OFFS, pack_y(pos, hz, cotangent))]
    inverse = jnp.pad(power_two(-first_exp), ((0, 0), (0, BLK - first_exp.shape[1]))).astype(jnp.bfloat16)

    blocks_z, blocks_y = CZ // BLK, CY // BLK
    count = first_exp.shape[1]
    by_y_z = first_exp.reshape(NY, NZ, 8, count)
    first_z = lax.dynamic_index_in_dim(by_y_z, y, 0, False)
    diff_z = (first_z - rz[:, 256 + CZ : 264 + CZ, :count].astype(jnp.int32)).reshape(64, count)
    diff_z = lax.dynamic_slice_in_dim(diff_z, blocks_z * z, blocks_z, 1)
    scale_z = jnp.repeat(power_two(diff_z), BLK, axis=1)
    by_step = jnp.stack([second_exp] + [q[256 + CY : 264 + CY, :count].astype(jnp.int32) for q in (q3, q2, q1)])
    second_y = by_step[(jnp.arange(NY) - y) % NY]
    diff_y = (lax.dynamic_index_in_dim(by_y_z, z, 1, False) - second_y).reshape(32, count)
    diff_y = lax.dynamic_slice_in_dim(diff_y, HALF // BLK + blocks_y * y, blocks_y, 1)
    scale_y = jnp.repeat(power_two(diff_y), BLK, axis=1)

    sy = sum_y(pos, inverse, hz, cotangent, q2, q1, q3)
    ry = lax.all_to_all(sy, "intra", 0, 0, axis_index_groups=Z_GROUPS, tiled=True)
    own, s2, s1, s3 = sum_z(pos, inverse, rz)
    t2, t1, t3 = [lax.ppermute(s, "intra", y_shift(step)) for step, s in zip(OFFS, (s2, s1, s3))]
    second = second_codes(own, t2, t1, t3, ry, scale_z, scale_y)

    received = lax.all_to_all(second, "inter", 0, 0, tiled=True)
    total = jnp.sum(received, axis=0, dtype=jnp.float32)
    rows = lax.ppermute(total, ("inter", "intra"), last_moves())
    my_exp = lax.dynamic_slice_in_dim(second_exp, group * blocks_z, blocks_z, 1)
    return rows * (jnp.repeat(power_two(my_exp), BLK, axis=1) * (1.0 / (NG * NM)))


def solution(mesh):
    return jax.shard_map(
        body,
        mesh=mesh,
        in_specs=(P(("inter", "intra"), None), P(("inter", "intra"), None), P(), P("intra", None)),
        out_specs=P("intra", "inter"),
        check_vma=False,
    )
```

```python
import jax
import jax.numpy as jnp
from jax import lax
from jax.experimental import pallas as pl
from jax.experimental.pallas import tpu as pltpu
from jax.sharding import PartitionSpec as P

BLK = 128
NY = 4
NZ = 8
NG = 16
NM = NY * NZ
HALF = 7168
CZ = HALF // NZ
CY = HALF // NY
OFFS = (2, 1, -1)
MAGIC = 12582912.0
Z_GROUPS = [[y * NZ + z for z in range(NZ)] for y in range(NY)]


def y_shift(step):
    return [(y * NZ + z, ((y + step) % NY) * NZ + z) for y in range(NY) for z in range(NZ)]


def last_moves():
    moves = []
    for group in range(NG):
        for y in range(NY):
            for z in range(NZ):
                if group < 8:
                    target = z * NM + y * NZ + group
                else:
                    target = (8 + 2 * y + group % 2) * NM + ((group - 8) // 2) * NZ + z
                moves.append((group * NM + y * NZ + z, target))
    return moves


def power_two(expo):
    total = jnp.zeros(expo.shape, jnp.float32)
    for power in range(-8, 9):
        total = total + jnp.where(expo == power, jnp.float32(2.0**power), jnp.float32(0.0))
    return total


def round_clip(values):
    return (jnp.clip(values, -127.0, 127.0) + MAGIC) - MAGIC


def pack_z_kernel(acts, exps, cot, out, held, padded, into, outof):
    loads = []
    for j in range(NZ):
        for b in range(CZ // BLK):
            column = j * CZ + b * BLK
            rows = pl.ds(256 + b * BLK, BLK)
            loads.append(
                pltpu.make_async_copy(cot.at[:, column : column + BLK], held.at[j, rows, :], into.at[len(loads)])
            )
    for load in loads:
        load.start()
    turned = acts[...].T
    padded[...] = jnp.zeros((16, BLK), jnp.float32)
    padded[0:8, 0 : exps.shape[1]] = exps[...].astype(jnp.float32)
    tail = padded[...].astype(jnp.bfloat16)
    for j in range(NZ):
        held[j, 0:256, :] = turned
        held[j, 256 + CZ : 256 + CZ + 16, :] = tail
    stores = [pltpu.make_async_copy(held.at[j], out.at[j], outof.at[j]) for j in range(NZ)]
    for j in range(NZ):
        for b in range(CZ // BLK):
            loads[j * (CZ // BLK) + b].wait()
        stores[j].start()
    for store in stores:
        store.wait()


def pack_z(acts, exps, cot):
    shape = (NZ, 256 + CZ + 16, BLK)
    any_spec = pl.BlockSpec(memory_space=pl.ANY)
    vmem_spec = pl.BlockSpec(memory_space=pltpu.VMEM)
    return pl.pallas_call(
        pack_z_kernel,
        out_shape=jax.ShapeDtypeStruct(shape, jnp.bfloat16),
        in_specs=[vmem_spec, vmem_spec, any_spec],
        out_specs=any_spec,
        scratch_shapes=[
            pltpu.VMEM(shape, jnp.bfloat16),
            pltpu.VMEM((16, BLK), jnp.float32),
            pltpu.SemaphoreType.DMA((HALF // BLK,)),
            pltpu.SemaphoreType.DMA((NZ,)),
        ],
        cost_estimate=pl.CostEstimate(flops=0, bytes_accessed=4000000, transcendentals=0),
    )(acts, exps, cot)


def pack_y_kernel(hz, cot, p2, p1, p3, held, into, outof):
    y = lax.axis_index("intra") // NZ
    loads, stores = [], []
    per = CY // BLK + 2
    for i, (step, out) in enumerate(zip(OFFS, (p2, p1, p3))):
        start = HALF + CY * lax.rem(y + step + NY, NY)
        moves = [(hz.at[0, 0:256], held.at[i, 0:256]), (hz.at[0, pl.ds(256 + CZ, 16)], held.at[i, pl.ds(256 + CY, 16)])]
        for b in range(CY // BLK):
            column = pl.multiple_of(start + b * BLK, BLK)
            moves.append((cot.at[:, pl.ds(column, BLK)], held.at[i, pl.ds(256 + b * BLK, BLK), :]))
        loads += [pltpu.make_async_copy(src, dst, into.at[i * per + k]) for k, (src, dst) in enumerate(moves)]
        stores.append(pltpu.make_async_copy(held.at[i], out, outof.at[i]))
    for load in loads:
        load.start()
    for i in range(3):
        for k in range(per):
            loads[i * per + k].wait()
        stores[i].start()
    for store in stores:
        store.wait()


def pack_y(hz, cot):
    any_spec = pl.BlockSpec(memory_space=pl.ANY)
    piece = jax.ShapeDtypeStruct((256 + CY + 16, BLK), jnp.bfloat16)
    return pl.pallas_call(
        pack_y_kernel,
        out_shape=[piece, piece, piece],
        in_specs=[any_spec, any_spec],
        out_specs=[any_spec] * 3,
        scratch_shapes=[
            pltpu.VMEM((3, 256 + CY + 16, BLK), jnp.bfloat16),
            pltpu.SemaphoreType.DMA((3 * (CY // BLK + 2),)),
            pltpu.SemaphoreType.DMA((3,)),
        ],
        cost_estimate=pl.CostEstimate(flops=0, bytes_accessed=3000000, transcendentals=0),
    )(hz, cot)


def spread(inverse, first_block, width):
    block = lax.broadcasted_iota(jnp.int32, (BLK, width), 0)
    column = lax.broadcasted_iota(jnp.int32, (BLK, width), 1)
    pick = jnp.where(block == first_block + column // BLK, 1.0, 0.0).astype(jnp.bfloat16)
    return jnp.dot(inverse, pick, preferred_element_type=jnp.float32)


def sum_y_kernel(pos, inverse, hz, cot, q2, q1, q3, out, lhs, own, sems):
    start = HALF + CY * pos[0]
    loads = [
        pltpu.make_async_copy(hz.at[0, 0:256], lhs, sems.at[0]),
        pltpu.make_async_copy(cot.at[:, pl.ds(pl.multiple_of(start, CY), CY)], own, sems.at[1]),
    ]
    for load in loads:
        load.start()
    for load in loads:
        load.wait()
    for i in range(CY // 256):
        scale = spread(inverse[...], HALF // BLK + pos[0] * (CY // BLK) + 2 * i, 256)
        local = jnp.dot(lhs[...], own[:, 256 * i : 256 * i + 256], preferred_element_type=jnp.float32)
        total = round_clip(local * scale)
        for part in (q2, q1, q3):
            row = 256 + 256 * i
            both = jnp.concatenate([part[row : row + BLK], part[row + BLK : row + 2 * BLK]], axis=1)
            local = jnp.dot(part[0:256], both, preferred_element_type=jnp.float32)
            total = total + round_clip(local * scale)
        for z in range(NZ):
            rows = [total[64 * y + 8 * z : 64 * y + 8 * z + 8] for y in range(NY)]
            out[z, :, 256 * i : 256 * i + 256] = jnp.concatenate(rows, axis=0).astype(jnp.int16)


def sum_y(pos, inverse, hz, cot, q2, q1, q3):
    any_spec = pl.BlockSpec(memory_space=pl.ANY)
    vmem_spec = pl.BlockSpec(memory_space=pltpu.VMEM)
    return pl.pallas_call(
        sum_y_kernel,
        out_shape=jax.ShapeDtypeStruct((NZ, 32, CY), jnp.int16),
        in_specs=[pl.BlockSpec(memory_space=pltpu.SMEM), vmem_spec, any_spec, any_spec] + [vmem_spec] * 3,
        out_specs=vmem_spec,
        scratch_shapes=[
            pltpu.VMEM((256, BLK), jnp.bfloat16),
            pltpu.VMEM((128, CY), jnp.bfloat16),
            pltpu.SemaphoreType.DMA((2,)),
        ],
        cost_estimate=pl.CostEstimate(flops=2 * 4 * 256 * 128 * CY, bytes_accessed=3000000, transcendentals=0),
    )(pos, inverse, hz, cot, q2, q1, q3)


def sum_z_kernel(pos, inverse, parts, own, s2, s1, s3, held, total_ref, sems):
    loads = [pltpu.make_async_copy(parts.at[:, 0:256], held.at[:, 0:256], sems.at[0])]
    for b in range(CZ // BLK):
        rows = pl.ds(256 + b * BLK, BLK)
        loads.append(pltpu.make_async_copy(parts.at[:, rows], held.at[:, rows], sems.at[1 + b]))
    for load in loads:
        load.start()
    loads[0].wait()
    for b in range(CZ // BLK):
        loads[1 + b].wait()
        scale = spread(inverse[...], pos[1] * (CZ // BLK) + b, BLK)
        for h in range(2):
            total = jnp.zeros((BLK, BLK), jnp.float32)
            for r in range(NZ):
                local = jnp.dot(
                    held[r, h * BLK : h * BLK + BLK],
                    held[r, 256 + b * BLK : 256 + b * BLK + BLK],
                    preferred_element_type=jnp.float32,
                )
                total = total + round_clip(local * scale[h * BLK : h * BLK + BLK])
            total_ref[h * BLK : h * BLK + BLK, b * BLK : b * BLK + BLK] = total
    for step, out in zip((0,) + OFFS, (own, s2, s1, s3)):
        start = 64 * lax.rem(pos[0] + step + NY, NY)
        out[...] = total_ref[pl.ds(pl.multiple_of(start, 64), 64), :].astype(jnp.int16)


def sum_z(pos, inverse, parts):
    vmem_spec = pl.BlockSpec(memory_space=pltpu.VMEM)
    return pl.pallas_call(
        sum_z_kernel,
        out_shape=[jax.ShapeDtypeStruct((64, CZ), jnp.int16)] * 4,
        in_specs=[pl.BlockSpec(memory_space=pltpu.SMEM), vmem_spec, pl.BlockSpec(memory_space=pl.ANY)],
        out_specs=[vmem_spec] * 4,
        scratch_shapes=[
            pltpu.VMEM((NZ, 256 + CZ, BLK), jnp.bfloat16),
            pltpu.VMEM((256, CZ), jnp.float32),
            pltpu.SemaphoreType.DMA((1 + CZ // BLK,)),
        ],
        cost_estimate=pl.CostEstimate(flops=2 * 8 * 256 * 128 * CZ, bytes_accessed=3000000, transcendentals=0),
    )(pos, inverse, parts)


def second_kernel(pos, first, second, rz, q2, q1, q3, own, s2, s1, s3, sy, out, tail_z, tail_y, diff, sems):
    y, z = pos[0], pos[1]
    loads = [pltpu.make_async_copy(rz.at[:, pl.ds(256 + CZ, 16)], tail_z, sems.at[0])]
    for i, part in enumerate((q3, q2, q1)):
        loads.append(pltpu.make_async_copy(part.at[pl.ds(256 + CY, 16)], tail_y.at[i], sems.at[1 + i]))
    for load in loads:
        load.start()
    for load in loads:
        load.wait()

    for r in range(NZ):
        rows = pl.ds(pl.multiple_of(64 * y + 8 * r, 8), 8)
        diff[8 * r : 8 * r + 8] = first[rows].astype(jnp.float32) - tail_z[r].astype(jnp.float32)[0:8]
    scale = spread(power_two(diff[...]).astype(jnp.bfloat16), z * (CZ // BLK), CZ)
    total = own[...].astype(jnp.int32)
    for part in (s2, s1, s3):
        total = total + part[...].astype(jnp.int32)
    codes = round_clip(total.astype(jnp.float32) * scale)
    for k in range(8):
        out[k] = codes[8 * k : 8 * k + 8].astype(jnp.bfloat16)

    for step in range(NY):
        member = lax.rem(y + step, NY)
        expo = second[...].astype(jnp.float32) if step == 0 else tail_y[step - 1].astype(jnp.float32)[0:8]
        rows = pl.ds(pl.multiple_of(64 * member + 8 * z, 8), 8)
        diff[pl.ds(pl.multiple_of(8 * member, 8), 8)] = first[rows].astype(jnp.float32) - expo
    factor = power_two(diff[0:32]).astype(jnp.bfloat16)
    for c in range(2):
        scale = spread(factor, HALF // BLK + y * (CY // BLK) + c * (CZ // BLK), CZ)
        total = sy[0, :, c * CZ : c * CZ + CZ].astype(jnp.int32)
        for r in range(1, NZ):
            total = total + sy[r, :, c * CZ : c * CZ + CZ].astype(jnp.int32)
        codes = round_clip(total.astype(jnp.float32) * scale)
        for k in range(NY):
            out[8 + 2 * k + c] = codes[8 * k : 8 * k + 8].astype(jnp.bfloat16)


def second_codes(pos, first, second, rz, q2, q1, q3, own, s2, s1, s3, sy):
    any_spec = pl.BlockSpec(memory_space=pl.ANY)
    vmem_spec = pl.BlockSpec(memory_space=pltpu.VMEM)
    return pl.pallas_call(
        second_kernel,
        out_shape=jax.ShapeDtypeStruct((NG, 8, CZ), jnp.bfloat16),
        in_specs=[pl.BlockSpec(memory_space=pltpu.SMEM), vmem_spec, vmem_spec] + [any_spec] * 4 + [vmem_spec] * 5,
        out_specs=vmem_spec,
        scratch_shapes=[
            pltpu.VMEM((NZ, 16, BLK), jnp.bfloat16),
            pltpu.VMEM((3, 16, BLK), jnp.bfloat16),
            pltpu.VMEM((64, BLK), jnp.float32),
            pltpu.SemaphoreType.DMA((4,)),
        ],
        cost_estimate=pl.CostEstimate(flops=4000000, bytes_accessed=2500000, transcendentals=0),
    )(pos, first, second, rz, q2, q1, q3, own, s2, s1, s3, sy)


def body(acts, cotangent, first_exp, second_exp):
    member = lax.axis_index("intra")
    group = lax.axis_index("inter")
    y, z = member // NZ, member % NZ
    pos = jnp.stack([y, z]).astype(jnp.int32)

    hz = pack_z(acts, second_exp, cotangent)
    rz = lax.all_to_all(hz, "intra", 0, 0, axis_index_groups=Z_GROUPS, tiled=True)
    q2, q1, q3 = [lax.ppermute(p, "intra", y_shift(step)) for step, p in zip(OFFS, pack_y(hz, cotangent))]
    room = ((0, 0), (0, BLK - first_exp.shape[1]))
    first, second = jnp.pad(first_exp, room), jnp.pad(second_exp, room)
    inverse = power_two(-first).astype(jnp.bfloat16)

    sy = sum_y(pos, inverse, hz, cotangent, q2, q1, q3)
    ry = lax.all_to_all(sy, "intra", 0, 0, axis_index_groups=Z_GROUPS, tiled=True)
    own, s2, s1, s3 = sum_z(pos, inverse, rz)
    t2, t1, t3 = [lax.ppermute(s, "intra", y_shift(step)) for step, s in zip(OFFS, (s2, s1, s3))]
    codes = second_codes(pos, first, second, rz, q2, q1, q3, own, t2, t1, t3, ry)

    received = lax.all_to_all(codes, "inter", 0, 0, tiled=True)
    total = jnp.sum(received, axis=0, dtype=jnp.float32)
    rows = lax.ppermute(total, ("inter", "intra"), last_moves())
    my_exp = lax.dynamic_slice_in_dim(second_exp, group * (CZ // BLK), CZ // BLK, 1)
    return rows * (jnp.repeat(power_two(my_exp), BLK, axis=1) * (1.0 / (NG * NM)))


def solution(mesh):
    return jax.shard_map(
        body,
        mesh=mesh,
        in_specs=(P(("inter", "intra"), None), P(("inter", "intra"), None), P(), P("intra", None)),
        out_specs=P("intra", "inter"),
        check_vma=False,
    )
```

```python
import jax
import jax.numpy as jnp
from jax import lax
from jax.experimental import pallas as pl
from jax.experimental.pallas import tpu as pltpu
from jax.sharding import PartitionSpec as P

BLK = 128
NY = 4
NZ = 8
NG = 16
NM = NY * NZ
HALF = 7168
CZ = HALF // NZ
CY = HALF // NY
OFFS = (2, 1, -1)
MAGIC = 12582912.0
SMALL = pltpu.CompilerParams(vmem_limit_bytes=8 * 1024 * 1024)
Z_GROUPS = [[y * NZ + z for z in range(NZ)] for y in range(NY)]


def y_shift(step):
    return [(y * NZ + z, ((y + step) % NY) * NZ + z) for y in range(NY) for z in range(NZ)]


def last_moves():
    moves = []
    for group in range(NG):
        for y in range(NY):
            for z in range(NZ):
                if group < 8:
                    target = z * NM + y * NZ + group
                else:
                    target = (8 + 2 * y + group % 2) * NM + ((group - 8) // 2) * NZ + z
                moves.append((group * NM + y * NZ + z, target))
    return moves


def power_two(expo):
    total = jnp.zeros(expo.shape, jnp.float32)
    for power in range(-8, 9):
        total = total + jnp.where(expo == power, jnp.float32(2.0**power), jnp.float32(0.0))
    return total


def in_vmem(*arrays):
    return [pltpu.with_memory_space_constraint(array, pltpu.VMEM) for array in arrays]


def place():
    member = lax.axis_index("intra")
    return member // NZ, lax.rem(member, NZ)


def round_clip(values):
    return (jnp.clip(values, -127.0, 127.0) + MAGIC) - MAGIC


def pack_z_kernel(acts, exps, cot, out, held, padded, into, outof):
    loads = []
    for j in range(NZ):
        for b in range(CZ // BLK):
            column = j * CZ + b * BLK
            rows = pl.ds(256 + b * BLK, BLK)
            loads.append(
                pltpu.make_async_copy(cot.at[:, column : column + BLK], held.at[j, rows, :], into.at[len(loads)])
            )
    for load in loads:
        load.start()
    turned = acts[...].T
    padded[...] = jnp.zeros((16, BLK), jnp.float32)
    padded[0:8, 0 : exps.shape[1]] = exps[...].astype(jnp.float32)
    tail = padded[...].astype(jnp.bfloat16)
    for j in range(NZ):
        held[j, 0:256, :] = turned
        held[j, 256 + CZ : 256 + CZ + 16, :] = tail
    stores = [pltpu.make_async_copy(held.at[j], out.at[j], outof.at[j]) for j in range(NZ)]
    for j in range(NZ):
        for b in range(CZ // BLK):
            loads[j * (CZ // BLK) + b].wait()
        stores[j].start()
    for store in stores:
        store.wait()


def pack_z(acts, exps, cot):
    shape = (NZ, 256 + CZ + 16, BLK)
    any_spec = pl.BlockSpec(memory_space=pl.ANY)
    vmem_spec = pl.BlockSpec(memory_space=pltpu.VMEM)
    return pl.pallas_call(
        pack_z_kernel,
        out_shape=jax.ShapeDtypeStruct(shape, jnp.bfloat16),
        in_specs=[vmem_spec, vmem_spec, any_spec],
        out_specs=any_spec,
        scratch_shapes=[
            pltpu.VMEM(shape, jnp.bfloat16),
            pltpu.VMEM((16, BLK), jnp.float32),
            pltpu.SemaphoreType.DMA((HALF // BLK,)),
            pltpu.SemaphoreType.DMA((NZ,)),
        ],
        cost_estimate=pl.CostEstimate(flops=0, bytes_accessed=4000000, transcendentals=0),
    )(acts, exps, cot)


def pack_y_kernel(hz, cot, p2, p1, p3, held, into, outof):
    y, _ = place()
    loads, stores = [], []
    per = CY // BLK + 2
    for i, (step, out) in enumerate(zip(OFFS, (p2, p1, p3))):
        start = HALF + CY * lax.rem(y + step + NY, NY)
        moves = [(hz.at[0, 0:256], held.at[i, 0:256]), (hz.at[0, pl.ds(256 + CZ, 16)], held.at[i, pl.ds(256 + CY, 16)])]
        for b in range(CY // BLK):
            column = pl.multiple_of(start + b * BLK, BLK)
            moves.append((cot.at[:, pl.ds(column, BLK)], held.at[i, pl.ds(256 + b * BLK, BLK), :]))
        loads += [pltpu.make_async_copy(src, dst, into.at[i * per + k]) for k, (src, dst) in enumerate(moves)]
        stores.append(pltpu.make_async_copy(held.at[i], out, outof.at[i]))
    for load in loads:
        load.start()
    for i in range(3):
        for k in range(per):
            loads[i * per + k].wait()
        stores[i].start()
    for store in stores:
        store.wait()


def pack_y(hz, cot):
    any_spec = pl.BlockSpec(memory_space=pl.ANY)
    piece = jax.ShapeDtypeStruct((256 + CY + 16, BLK), jnp.bfloat16)
    return pl.pallas_call(
        pack_y_kernel,
        out_shape=[piece, piece, piece],
        in_specs=[any_spec, any_spec],
        out_specs=[any_spec] * 3,
        scratch_shapes=[
            pltpu.VMEM((3, 256 + CY + 16, BLK), jnp.bfloat16),
            pltpu.SemaphoreType.DMA((3 * (CY // BLK + 2),)),
            pltpu.SemaphoreType.DMA((3,)),
        ],
        cost_estimate=pl.CostEstimate(flops=0, bytes_accessed=3000000, transcendentals=0),
    )(hz, cot)


def spread(inverse, first_block, width):
    block = lax.broadcasted_iota(jnp.int32, (BLK, width), 0)
    column = lax.broadcasted_iota(jnp.int32, (BLK, width), 1)
    pick = jnp.where(block == first_block + column // BLK, 1.0, 0.0).astype(jnp.bfloat16)
    return jnp.dot(inverse, pick, preferred_element_type=jnp.float32)


def codes_y(lhs, part, i, scale):
    row = 256 + 256 * i
    both = jnp.concatenate([part[row : row + BLK], part[row + BLK : row + 2 * BLK]], axis=1)
    return round_clip(jnp.dot(lhs, both, preferred_element_type=jnp.float32) * scale)


def early_y_kernel(inverse, hz, cot, q2, out, lhs, own, sems):
    y, _ = place()
    start = HALF + CY * y
    loads = [
        pltpu.make_async_copy(hz.at[0, 0:256], lhs, sems.at[0]),
        pltpu.make_async_copy(cot.at[:, pl.ds(pl.multiple_of(start, CY), CY)], own, sems.at[1]),
    ]
    for load in loads:
        load.start()
    for load in loads:
        load.wait()
    for i in range(CY // 256):
        columns = slice(256 * i, 256 * i + 256)
        scale = spread(inverse[...], HALF // BLK + y * (CY // BLK) + 2 * i, 256)
        local = jnp.dot(lhs[...], own[:, columns], preferred_element_type=jnp.float32)
        total = round_clip(local * scale) + codes_y(q2[0:256], q2, i, scale)
        out[:, columns] = total.astype(jnp.bfloat16)


def early_y(inverse, hz, cot, q2):
    any_spec = pl.BlockSpec(memory_space=pl.ANY)
    vmem_spec = pl.BlockSpec(memory_space=pltpu.VMEM)
    return pl.pallas_call(
        early_y_kernel,
        out_shape=jax.ShapeDtypeStruct((256, CY), jnp.bfloat16),
        in_specs=[vmem_spec, any_spec, any_spec, vmem_spec],
        out_specs=vmem_spec,
        scratch_shapes=[
            pltpu.VMEM((256, BLK), jnp.bfloat16),
            pltpu.VMEM((128, CY), jnp.bfloat16),
            pltpu.SemaphoreType.DMA((2,)),
        ],
        compiler_params=SMALL,
        cost_estimate=pl.CostEstimate(flops=2 * 2 * 256 * 128 * CY, bytes_accessed=2000000, transcendentals=0),
    )(inverse, hz, cot, *in_vmem(q2))


def late_y_kernel(inverse, first, second, early, q2, q1, q3, out, factor, diff):
    y, z = place()
    for i in range(CY // 256):
        columns = slice(256 * i, 256 * i + 256)
        scale = spread(inverse[...], HALF // BLK + y * (CY // BLK) + 2 * i, 256)
        total = early[:, columns].astype(jnp.float32)
        total = total + codes_y(q1[0:256], q1, i, scale) + codes_y(q3[0:256], q3, i, scale)
        for k in range(NZ):
            rows = [total[64 * j + 8 * k : 64 * j + 8 * k + 8] for j in range(NY)]
            out[k, :, columns] = jnp.concatenate(rows, axis=0).astype(jnp.int16)
    for step in range(NY):
        member = lax.rem(y + step, NY)
        expo = second[...].astype(jnp.float32)
        if step > 0:
            expo = (q3, q2, q1)[step - 1][256 + CY : 256 + CY + 16].astype(jnp.float32)[0:8]
        rows = pl.ds(pl.multiple_of(64 * member + 8 * z, 8), 8)
        diff[pl.ds(pl.multiple_of(8 * member, 8), 8)] = first[rows].astype(jnp.float32) - expo
    factor[...] = power_two(diff[...])


def late_y(inverse, first, second, early, q2, q1, q3):
    vmem_spec = pl.BlockSpec(memory_space=pltpu.VMEM)
    return pl.pallas_call(
        late_y_kernel,
        out_shape=[
            jax.ShapeDtypeStruct((NZ, 32, CY), jnp.int16),
            jax.ShapeDtypeStruct((32, BLK), jnp.float32),
        ],
        in_specs=[vmem_spec] * 7,
        out_specs=[vmem_spec] * 2,
        scratch_shapes=[pltpu.VMEM((32, BLK), jnp.float32)],
        compiler_params=SMALL,
        cost_estimate=pl.CostEstimate(flops=2 * 2 * 256 * 128 * CY, bytes_accessed=2000000, transcendentals=0),
    )(inverse, first, second, *in_vmem(early, q2, q1, q3))


def sum_z_kernel(inverse, first, parts, own, s2, s1, s3, factor, total_ref, diff):
    y, z = place()
    for b in range(CZ // BLK):
        scale = spread(inverse[...], z * (CZ // BLK) + b, BLK)
        for h in range(2):
            total = jnp.zeros((BLK, BLK), jnp.float32)
            for r in range(NZ):
                local = jnp.dot(
                    parts[r, h * BLK : h * BLK + BLK],
                    parts[r, 256 + b * BLK : 256 + b * BLK + BLK],
                    preferred_element_type=jnp.float32,
                )
                total = total + round_clip(local * scale[h * BLK : h * BLK + BLK])
            total_ref[h * BLK : h * BLK + BLK, b * BLK : b * BLK + BLK] = total
    for step, out in zip((0,) + OFFS, (own, s2, s1, s3)):
        start = 64 * lax.rem(y + step + NY, NY)
        out[...] = total_ref[pl.ds(pl.multiple_of(start, 64), 64), :].astype(jnp.int16)
    for r in range(NZ):
        rows = pl.ds(pl.multiple_of(64 * y + 8 * r, 8), 8)
        expo = parts[r, 256 + CZ : 256 + CZ + 16].astype(jnp.float32)[0:8]
        diff[8 * r : 8 * r + 8] = first[rows].astype(jnp.float32) - expo
    factor[...] = power_two(diff[...])


def sum_z(inverse, first, parts):
    vmem_spec = pl.BlockSpec(memory_space=pltpu.VMEM)
    return pl.pallas_call(
        sum_z_kernel,
        out_shape=[jax.ShapeDtypeStruct((64, CZ), jnp.int16)] * 4 + [jax.ShapeDtypeStruct((64, BLK), jnp.float32)],
        in_specs=[vmem_spec] * 3,
        out_specs=[vmem_spec] * 5,
        scratch_shapes=[pltpu.VMEM((256, CZ), jnp.float32), pltpu.VMEM((64, BLK), jnp.float32)],
        compiler_params=SMALL,
        cost_estimate=pl.CostEstimate(flops=2 * 8 * 256 * 128 * CZ, bytes_accessed=3000000, transcendentals=0),
    )(inverse, first, *in_vmem(parts))


def second_kernel(factor_z, factor_y, own, s2, s1, s3, sy, out):
    y, z = place()
    scale = spread(factor_z[...].astype(jnp.bfloat16), z * (CZ // BLK), CZ)
    total = own[...].astype(jnp.int32)
    for part in (s2, s1, s3):
        total = total + part[...].astype(jnp.int32)
    codes = round_clip(total.astype(jnp.float32) * scale)
    for k in range(8):
        out[k] = codes[8 * k : 8 * k + 8].astype(jnp.bfloat16)
    scale = spread(factor_y[...].astype(jnp.bfloat16), HALF // BLK + y * (CY // BLK), CY)
    total = sy[0].astype(jnp.int32)
    for r in range(1, NZ):
        total = total + sy[r].astype(jnp.int32)
    codes = round_clip(total.astype(jnp.float32) * scale)
    for k in range(NY):
        for c in range(2):
            out[8 + 2 * k + c] = codes[8 * k : 8 * k + 8, c * CZ : c * CZ + CZ].astype(jnp.bfloat16)


def second_codes(factor_z, factor_y, *arrays):
    vmem_spec = pl.BlockSpec(memory_space=pltpu.VMEM)
    return pl.pallas_call(
        second_kernel,
        out_shape=jax.ShapeDtypeStruct((NG, 8, CZ), jnp.bfloat16),
        in_specs=[vmem_spec] * 7,
        out_specs=vmem_spec,
        compiler_params=SMALL,
        cost_estimate=pl.CostEstimate(flops=4000000, bytes_accessed=2500000, transcendentals=0),
    )(*in_vmem(factor_z, factor_y, *arrays))


def body(acts, cotangent, first_exp, second_exp):
    group = lax.axis_index("inter")
    far = pltpu.with_memory_space_constraint(cotangent, pltpu.HBM)

    hz = pack_z(acts, second_exp, far)
    rz = lax.all_to_all(hz, "intra", 0, 0, axis_index_groups=Z_GROUPS, tiled=True)
    q2, q1, q3 = [lax.ppermute(p, "intra", y_shift(step)) for step, p in zip(OFFS, pack_y(hz, far))]
    room = ((0, 0), (0, BLK - first_exp.shape[1]))
    first, second = jnp.pad(first_exp, room), jnp.pad(second_exp, room)
    inverse = power_two(-first).astype(jnp.bfloat16)

    early = early_y(inverse, hz, far, q2)
    sy, factor_y = late_y(inverse, first, second, early, q2, q1, q3)
    ry = lax.all_to_all(sy, "intra", 0, 0, axis_index_groups=Z_GROUPS, tiled=True)
    own, s2, s1, s3, factor_z = sum_z(inverse, first, rz)
    t2, t1, t3 = [lax.ppermute(s, "intra", y_shift(step)) for step, s in zip(OFFS, (s2, s1, s3))]
    codes = second_codes(factor_z, factor_y, own, t2, t1, t3, ry)

    received = lax.all_to_all(codes, "inter", 0, 0, tiled=True)
    total = jnp.sum(received, axis=0, dtype=jnp.float32)
    rows = lax.ppermute(total, ("inter", "intra"), last_moves())
    my_exp = lax.dynamic_slice_in_dim(second_exp, group * (CZ // BLK), CZ // BLK, 1)
    return rows * (jnp.repeat(power_two(my_exp), BLK, axis=1) * (1.0 / (NG * NM)))


def solution(mesh):
    return jax.shard_map(
        body,
        mesh=mesh,
        in_specs=(P(("inter", "intra"), None), P(("inter", "intra"), None), P(), P("intra", None)),
        out_specs=P("intra", "inter"),
        check_vma=False,
    )
```

```python
import jax
import jax.numpy as jnp
from jax import lax
from jax.experimental import pallas as pl
from jax.experimental.pallas import tpu as pltpu
from jax.sharding import PartitionSpec as P

BLK = 128
NY = 4
NZ = 8
NG = 16
NM = NY * NZ
HALF = 7168
CZ = HALF // NZ
CY = HALF // NY
OFFS = (2, 1, -1)
MAGIC = 12582912.0
SMALL = pltpu.CompilerParams(vmem_limit_bytes=8 * 1024 * 1024)
Z_GROUPS = [[y * NZ + z for z in range(NZ)] for y in range(NY)]


def y_shift(step):
    return [(y * NZ + z, ((y + step) % NY) * NZ + z) for y in range(NY) for z in range(NZ)]


def last_moves():
    moves = []
    for group in range(NG):
        for y in range(NY):
            for z in range(NZ):
                if group < 8:
                    target = z * NM + y * NZ + group
                else:
                    target = (8 + 2 * y + group % 2) * NM + ((group - 8) // 2) * NZ + z
                moves.append((group * NM + y * NZ + z, target))
    return moves


def power_two(expo):
    total = jnp.zeros(expo.shape, jnp.float32)
    for power in range(-8, 9):
        total = total + jnp.where(expo == power, jnp.float32(2.0**power), jnp.float32(0.0))
    return total


def in_vmem(*arrays):
    return [pltpu.with_memory_space_constraint(array, pltpu.VMEM) for array in arrays]


def in_hbm(*arrays):
    return [pltpu.with_memory_space_constraint(array, pltpu.HBM) for array in arrays]


def place():
    member = lax.axis_index("intra")
    return member // NZ, lax.rem(member, NZ)


def round_clip(values):
    return (jnp.clip(values, -127.0, 127.0) + MAGIC) - MAGIC


def pack_z_kernel(acts, exps, cot, out, wide, held, acts_here, exps_here, padded, into, outof):
    loads = [pltpu.make_async_copy(cot.at[:, j * CZ : (j + 1) * CZ], wide.at[j], into.at[j]) for j in range(NZ)]
    stores = [pltpu.make_async_copy(held.at[j], out.at[j], outof.at[j]) for j in range(NZ)]
    small = [
        pltpu.make_async_copy(acts, acts_here, into.at[NZ]),
        pltpu.make_async_copy(exps, exps_here, into.at[NZ + 1]),
    ]
    for load in small + loads:
        load.start()
    padded[...] = jnp.zeros((16, BLK), jnp.float32)
    for load in small:
        load.wait()
    turned = acts_here[...].T
    padded[0:8, 0 : exps.shape[1]] = exps_here[...].astype(jnp.float32)
    tail = padded[...].astype(jnp.bfloat16)
    for j in range(NZ):
        held[j, 0:256, :] = turned
        held[j, 256 + CZ : 256 + CZ + 16, :] = tail
        loads[j].wait()
        for b in range(CZ // BLK):
            held[j, 256 + b * BLK : 256 + b * BLK + BLK, :] = wide[j, :, b * BLK : b * BLK + BLK]
        stores[j].start()
    for store in stores:
        store.wait()


def pack_z(acts, exps, cot):
    shape = (NZ, 256 + CZ + 16, BLK)
    any_spec = pl.BlockSpec(memory_space=pl.ANY)
    return pl.pallas_call(
        pack_z_kernel,
        out_shape=jax.ShapeDtypeStruct(shape, jnp.bfloat16),
        in_specs=[any_spec, any_spec, any_spec],
        out_specs=any_spec,
        scratch_shapes=[
            pltpu.VMEM((NZ, 128, CZ), jnp.bfloat16),
            pltpu.VMEM(shape, jnp.bfloat16),
            pltpu.VMEM(acts.shape, jnp.bfloat16),
            pltpu.VMEM(exps.shape, jnp.int32),
            pltpu.VMEM((16, BLK), jnp.float32),
            pltpu.SemaphoreType.DMA((NZ + 2,)),
            pltpu.SemaphoreType.DMA((NZ,)),
        ],
        compiler_params=SMALL,
        cost_estimate=pl.CostEstimate(flops=0, bytes_accessed=4000000, transcendentals=0),
    )(*in_hbm(acts, exps, cot))


def pack_y_kernel(hz, cot, p2, p1, p3, wide, held, into, outof):
    y, _ = place()
    loads, stores = [], []
    for i, (step, out) in enumerate(zip(OFFS, (p2, p1, p3))):
        start = pl.multiple_of(HALF + CY * lax.rem(y + step + NY, NY), CY)
        moves = (
            (cot.at[:, pl.ds(start, CY)], wide.at[i]),
            (hz.at[0, 0:256], held.at[i, 0:256]),
            (hz.at[0, pl.ds(256 + CZ, 16)], held.at[i, pl.ds(256 + CY, 16)]),
        )
        loads += [pltpu.make_async_copy(src, dst, into.at[3 * i + k]) for k, (src, dst) in enumerate(moves)]
        stores.append(pltpu.make_async_copy(held.at[i], out, outof.at[i]))
    for load in loads:
        load.start()
    for i in range(3):
        for k in range(3):
            loads[3 * i + k].wait()
        for b in range(CY // BLK):
            held[i, 256 + b * BLK : 256 + b * BLK + BLK, :] = wide[i, :, b * BLK : b * BLK + BLK]
        stores[i].start()
    for store in stores:
        store.wait()


def pack_y(hz, cot):
    any_spec = pl.BlockSpec(memory_space=pl.ANY)
    piece = jax.ShapeDtypeStruct((256 + CY + 16, BLK), jnp.bfloat16)
    return pl.pallas_call(
        pack_y_kernel,
        out_shape=[piece, piece, piece],
        in_specs=[any_spec, any_spec],
        out_specs=[any_spec] * 3,
        scratch_shapes=[
            pltpu.VMEM((3, 128, CY), jnp.bfloat16),
            pltpu.VMEM((3, 256 + CY + 16, BLK), jnp.bfloat16),
            pltpu.SemaphoreType.DMA((9,)),
            pltpu.SemaphoreType.DMA((3,)),
        ],
        compiler_params=SMALL,
        cost_estimate=pl.CostEstimate(flops=0, bytes_accessed=3000000, transcendentals=0),
    )(hz, cot)


def spread(inverse, first_block, width):
    block = lax.broadcasted_iota(jnp.int32, (BLK, width), 0)
    column = lax.broadcasted_iota(jnp.int32, (BLK, width), 1)
    pick = jnp.where(block == first_block + column // BLK, 1.0, 0.0).astype(jnp.bfloat16)
    return jnp.dot(inverse, pick, preferred_element_type=jnp.float32)


def codes_y(lhs, part, i, scale):
    row = 256 + 256 * i
    both = jnp.concatenate([part[row : row + BLK], part[row + BLK : row + 2 * BLK]], axis=1)
    return round_clip(jnp.dot(lhs, both, preferred_element_type=jnp.float32) * scale)


def early_y_kernel(turned, hz, cot, q2, out, inverse, first, second, lhs, own, expo, sems):
    y, _ = place()
    start = HALF + CY * y
    loads = [
        pltpu.make_async_copy(hz.at[0, 0:256], lhs, sems.at[0]),
        pltpu.make_async_copy(hz.at[0, pl.ds(256 + CZ, 16)], expo, sems.at[1]),
        pltpu.make_async_copy(cot.at[:, pl.ds(pl.multiple_of(start, CY), CY)], own, sems.at[2]),
    ]
    for load in loads:
        load.start()
    count = turned.shape[0]
    exponent = jnp.concatenate([turned[...].astype(jnp.float32), jnp.zeros((BLK - count, 256), jnp.float32)], axis=0).T
    first[...] = exponent
    inverse[...] = power_two(-exponent).astype(jnp.bfloat16)
    for load in loads:
        load.wait()
    second[...] = expo[...].astype(jnp.float32)[0:8]
    for i in range(CY // 256):
        columns = slice(256 * i, 256 * i + 256)
        scale = spread(inverse[...], HALF // BLK + y * (CY // BLK) + 2 * i, 256)
        local = jnp.dot(lhs[...], own[:, columns], preferred_element_type=jnp.float32)
        total = round_clip(local * scale) + codes_y(q2[0:256], q2, i, scale)
        out[:, columns] = total.astype(jnp.bfloat16)


def early_y(turned, hz, cot, q2):
    any_spec = pl.BlockSpec(memory_space=pl.ANY)
    vmem_spec = pl.BlockSpec(memory_space=pltpu.VMEM)
    return pl.pallas_call(
        early_y_kernel,
        out_shape=[
            jax.ShapeDtypeStruct((256, CY), jnp.bfloat16),
            jax.ShapeDtypeStruct((256, BLK), jnp.bfloat16),
            jax.ShapeDtypeStruct((256, BLK), jnp.float32),
            jax.ShapeDtypeStruct((8, BLK), jnp.float32),
        ],
        in_specs=[vmem_spec, any_spec, any_spec, vmem_spec],
        out_specs=[vmem_spec] * 4,
        scratch_shapes=[
            pltpu.VMEM((256, BLK), jnp.bfloat16),
            pltpu.VMEM((128, CY), jnp.bfloat16),
            pltpu.VMEM((16, BLK), jnp.bfloat16),
            pltpu.SemaphoreType.DMA((3,)),
        ],
        compiler_params=SMALL,
        cost_estimate=pl.CostEstimate(flops=2 * 2 * 256 * 128 * CY, bytes_accessed=2000000, transcendentals=0),
    )(turned, hz, cot, *in_vmem(q2))


def late_y_kernel(inverse, first, second, early, q2, q1, q3, out, factor, diff, sums, sems):
    y, z = place()
    stores = []
    for i in range(CY // 256):
        columns = slice(256 * i, 256 * i + 256)
        scale = spread(inverse[...], HALF // BLK + y * (CY // BLK) + 2 * i, 256)
        total = early[:, columns].astype(jnp.float32)
        total = total + codes_y(q1[0:256], q1, i, scale) + codes_y(q3[0:256], q3, i, scale)
        for k in range(NZ):
            rows = [total[64 * j + 8 * k : 64 * j + 8 * k + 8] for j in range(NY)]
            sums[k, :, columns] = jnp.concatenate(rows, axis=0).astype(jnp.int16)
        stores.append(pltpu.make_async_copy(sums.at[:, :, columns], out.at[:, :, columns], sems.at[i]))
        stores[i].start()
    for step in range(NY):
        member = lax.rem(y + step, NY)
        expo = second[...]
        if step > 0:
            expo = (q3, q2, q1)[step - 1][256 + CY : 256 + CY + 16].astype(jnp.float32)[0:8]
        rows = pl.ds(pl.multiple_of(64 * member + 8 * z, 8), 8)
        diff[pl.ds(pl.multiple_of(8 * member, 8), 8)] = first[rows] - expo
    factor[...] = power_two(diff[...])
    for store in stores:
        store.wait()


def late_y(inverse, first, second, early, q2, q1, q3):
    vmem_spec = pl.BlockSpec(memory_space=pltpu.VMEM)
    shape = (NZ, 32, CY)
    return pl.pallas_call(
        late_y_kernel,
        out_shape=[pltpu.HBM(shape, jnp.int16), jax.ShapeDtypeStruct((32, BLK), jnp.float32)],
        in_specs=[vmem_spec] * 7,
        out_specs=[pl.BlockSpec(memory_space=pl.ANY), vmem_spec],
        scratch_shapes=[
            pltpu.VMEM((32, BLK), jnp.float32),
            pltpu.VMEM(shape, jnp.int16),
            pltpu.SemaphoreType.DMA((CY // 256,)),
        ],
        compiler_params=SMALL,
        cost_estimate=pl.CostEstimate(flops=2 * 2 * 256 * 128 * CY, bytes_accessed=2000000, transcendentals=0),
    )(inverse, first, second, *in_vmem(early, q2, q1, q3))


def sum_z_kernel(inverse, first, parts, own, s2, s1, s3, factor, total_ref, diff):
    y, z = place()
    for b in range(CZ // BLK):
        scale = spread(inverse[...], z * (CZ // BLK) + b, BLK)
        for h in range(2):
            total = jnp.zeros((BLK, BLK), jnp.float32)
            for r in range(NZ):
                local = jnp.dot(
                    parts[r, h * BLK : h * BLK + BLK],
                    parts[r, 256 + b * BLK : 256 + b * BLK + BLK],
                    preferred_element_type=jnp.float32,
                )
                total = total + round_clip(local * scale[h * BLK : h * BLK + BLK])
            total_ref[h * BLK : h * BLK + BLK, b * BLK : b * BLK + BLK] = total
    for step, out in zip((0,) + OFFS, (own, s2, s1, s3)):
        start = 64 * lax.rem(y + step + NY, NY)
        out[...] = total_ref[pl.ds(pl.multiple_of(start, 64), 64), :].astype(jnp.int16)
    for r in range(NZ):
        rows = pl.ds(pl.multiple_of(64 * y + 8 * r, 8), 8)
        expo = parts[r, 256 + CZ : 256 + CZ + 16].astype(jnp.float32)[0:8]
        diff[8 * r : 8 * r + 8] = first[rows] - expo
    factor[...] = power_two(diff[...])


def sum_z(inverse, first, parts):
    vmem_spec = pl.BlockSpec(memory_space=pltpu.VMEM)
    return pl.pallas_call(
        sum_z_kernel,
        out_shape=[pltpu.HBM((64, CZ), jnp.int16)]
        + [jax.ShapeDtypeStruct((64, CZ), jnp.int16)] * 3
        + [jax.ShapeDtypeStruct((64, BLK), jnp.float32)],
        in_specs=[vmem_spec] * 3,
        out_specs=[vmem_spec] * 5,
        scratch_shapes=[pltpu.VMEM((256, CZ), jnp.float32), pltpu.VMEM((64, BLK), jnp.float32)],
        compiler_params=SMALL,
        cost_estimate=pl.CostEstimate(flops=2 * 8 * 256 * 128 * CZ, bytes_accessed=3000000, transcendentals=0),
    )(inverse, first, *in_vmem(parts))


def second_kernel(factor_z, factor_y, own, s2, s1, s3, sy, out, own_here, sem):
    y, z = place()
    load = pltpu.make_async_copy(own, own_here, sem)
    load.start()
    scale = spread(factor_y[...].astype(jnp.bfloat16), HALF // BLK + y * (CY // BLK), CY)
    total = sy[0].astype(jnp.int32)
    for r in range(1, NZ):
        total = total + sy[r].astype(jnp.int32)
    codes = round_clip(total.astype(jnp.float32) * scale)
    for k in range(NY):
        for c in range(2):
            out[8 + 2 * k + c] = codes[8 * k : 8 * k + 8, c * CZ : c * CZ + CZ].astype(jnp.bfloat16)
    scale = spread(factor_z[...].astype(jnp.bfloat16), z * (CZ // BLK), CZ)
    total = s2[...].astype(jnp.int32) + s1[...].astype(jnp.int32) + s3[...].astype(jnp.int32)
    load.wait()
    total = total + own_here[...].astype(jnp.int32)
    codes = round_clip(total.astype(jnp.float32) * scale)
    for k in range(8):
        out[k] = codes[8 * k : 8 * k + 8].astype(jnp.bfloat16)


def second_codes(factor_z, factor_y, own, *arrays):
    vmem_spec = pl.BlockSpec(memory_space=pltpu.VMEM)
    return pl.pallas_call(
        second_kernel,
        out_shape=jax.ShapeDtypeStruct((NG, 8, CZ), jnp.bfloat16),
        in_specs=[vmem_spec, vmem_spec, pl.BlockSpec(memory_space=pl.ANY)] + [vmem_spec] * 4,
        out_specs=vmem_spec,
        scratch_shapes=[pltpu.VMEM((64, CZ), jnp.int16), pltpu.SemaphoreType.DMA],
        compiler_params=SMALL,
        cost_estimate=pl.CostEstimate(flops=4000000, bytes_accessed=2500000, transcendentals=0),
    )(*in_vmem(factor_z, factor_y), *in_hbm(own), *in_vmem(*arrays))


def body(acts, cotangent, first_exp, second_exp):
    group = lax.axis_index("inter")
    (far,) = in_hbm(cotangent)

    hz = pack_z(acts, second_exp, far)
    rz = lax.all_to_all(hz, "intra", 0, 0, axis_index_groups=Z_GROUPS, tiled=True)
    (near,) = in_hbm(hz)
    q2, q1, q3 = [lax.ppermute(p, "intra", y_shift(step)) for step, p in zip(OFFS, pack_y(near, far))]
    early, inverse, first, second = early_y(first_exp.T, near, far, q2)
    sy, factor_y = late_y(inverse, first, second, early, q2, q1, q3)
    ry = lax.all_to_all(sy, "intra", 0, 0, axis_index_groups=Z_GROUPS, tiled=True)
    own, s2, s1, s3, factor_z = sum_z(inverse, first, rz)
    t2, t1, t3 = [lax.ppermute(s, "intra", y_shift(step)) for step, s in zip(OFFS, (s2, s1, s3))]
    codes = second_codes(factor_z, factor_y, own, t2, t1, t3, ry)

    received = lax.all_to_all(codes, "inter", 0, 0, tiled=True)
    total = jnp.sum(received, axis=0, dtype=jnp.float32)
    rows = lax.ppermute(total, ("inter", "intra"), last_moves())
    my_exp = lax.dynamic_slice_in_dim(second_exp, group * (CZ // BLK), CZ // BLK, 1)
    return rows * (jnp.repeat(power_two(my_exp), BLK, axis=1) * (1.0 / (NG * NM)))


def solution(mesh):
    return jax.shard_map(
        body,
        mesh=mesh,
        in_specs=(P(("inter", "intra"), None), P(("inter", "intra"), None), P(), P("intra", None)),
        out_specs=P("intra", "inter"),
        check_vma=False,
    )
```

```python
import jax
import jax.numpy as jnp
from jax import lax
from jax.experimental import pallas as pl
from jax.experimental.pallas import tpu as pltpu
from jax.sharding import PartitionSpec as P

BLK = 128
NY = 4
NZ = 8
NG = 16
NM = NY * NZ
HALF = 7168
CZ = HALF // NZ
CY = HALF // NY
OFFS = (2, 1, -1)
MAGIC = 12582912.0
SMALL = pltpu.CompilerParams(vmem_limit_bytes=8 * 1024 * 1024)
FIRST_Z = 5
Z_ORDER = [(FIRST_Z + i) % NZ for i in range(NZ)]
Z_GROUPS = [[y * NZ + z for z in Z_ORDER] for y in range(NY)]


def y_shift(step):
    return [(y * NZ + z, ((y + step) % NY) * NZ + z) for y in range(NY) for z in range(NZ)]


def last_moves():
    moves = []
    for group in range(NG):
        for y in range(NY):
            for z in range(NZ):
                if group < 8:
                    target = z * NM + y * NZ + group
                else:
                    target = (8 + 2 * y + group % 2) * NM + ((group - 8) // 2) * NZ + z
                moves.append((group * NM + y * NZ + z, target))
    return moves


def power_two(expo):
    total = jnp.zeros(expo.shape, jnp.float32)
    for power in range(-8, 9):
        total = total + jnp.where(expo == power, jnp.float32(2.0**power), jnp.float32(0.0))
    return total


def in_vmem(*arrays):
    return [pltpu.with_memory_space_constraint(array, pltpu.VMEM) for array in arrays]


def in_hbm(*arrays):
    return [pltpu.with_memory_space_constraint(array, pltpu.HBM) for array in arrays]


def place():
    member = lax.axis_index("intra")
    return member // NZ, lax.rem(member, NZ)


def round_clip(values):
    return (jnp.clip(values, -127.0, 127.0) + MAGIC) - MAGIC


def pack_z_kernel(acts, exps, cot, out, wide, held, acts_here, exps_here, padded, into, outof):
    loads = [
        pltpu.make_async_copy(cot.at[:, z * CZ : (z + 1) * CZ], wide.at[j], into.at[j]) for j, z in enumerate(Z_ORDER)
    ]
    stores = [pltpu.make_async_copy(held.at[j], out.at[j], outof.at[j]) for j in range(NZ)]
    small = [
        pltpu.make_async_copy(acts, acts_here, into.at[NZ]),
        pltpu.make_async_copy(exps, exps_here, into.at[NZ + 1]),
    ]
    for load in small + loads:
        load.start()
    padded[...] = jnp.zeros((16, BLK), jnp.float32)
    for load in small:
        load.wait()
    turned = acts_here[...].T
    padded[0:8, 0 : exps.shape[1]] = exps_here[...].astype(jnp.float32)
    tail = padded[...].astype(jnp.bfloat16)
    for j in range(NZ):
        held[j, 0:256, :] = turned
        held[j, 256 + CZ : 256 + CZ + 16, :] = tail
        loads[j].wait()
        for b in range(CZ // BLK):
            held[j, 256 + b * BLK : 256 + b * BLK + BLK, :] = wide[j, :, b * BLK : b * BLK + BLK]
        stores[j].start()
    for store in stores:
        store.wait()


def pack_z(acts, exps, cot):
    shape = (NZ, 256 + CZ + 16, BLK)
    any_spec = pl.BlockSpec(memory_space=pl.ANY)
    return pl.pallas_call(
        pack_z_kernel,
        out_shape=jax.ShapeDtypeStruct(shape, jnp.bfloat16),
        in_specs=[any_spec, any_spec, any_spec],
        out_specs=any_spec,
        scratch_shapes=[
            pltpu.VMEM((NZ, 128, CZ), jnp.bfloat16),
            pltpu.VMEM(shape, jnp.bfloat16),
            pltpu.VMEM(acts.shape, jnp.bfloat16),
            pltpu.VMEM(exps.shape, jnp.int32),
            pltpu.VMEM((16, BLK), jnp.float32),
            pltpu.SemaphoreType.DMA((NZ + 2,)),
            pltpu.SemaphoreType.DMA((NZ,)),
        ],
        compiler_params=SMALL,
        cost_estimate=pl.CostEstimate(flops=0, bytes_accessed=4000000, transcendentals=0),
    )(*in_hbm(acts, exps, cot))


def pack_y_kernel(hz, cot, p2, p1, p3, wide, held, into, outof):
    y, _ = place()
    loads, stores = [], []
    for i, (step, out) in enumerate(zip(OFFS, (p2, p1, p3))):
        start = pl.multiple_of(HALF + CY * lax.rem(y + step + NY, NY), CY)
        moves = (
            (cot.at[:, pl.ds(start, CY)], wide.at[i]),
            (hz.at[0, 0:256], held.at[i, 0:256]),
            (hz.at[0, pl.ds(256 + CZ, 16)], held.at[i, pl.ds(256 + CY, 16)]),
        )
        loads += [pltpu.make_async_copy(src, dst, into.at[3 * i + k]) for k, (src, dst) in enumerate(moves)]
        stores.append(pltpu.make_async_copy(held.at[i], out, outof.at[i]))
    for load in loads:
        load.start()
    for i in range(3):
        for k in range(3):
            loads[3 * i + k].wait()
        for b in range(CY // BLK):
            held[i, 256 + b * BLK : 256 + b * BLK + BLK, :] = wide[i, :, b * BLK : b * BLK + BLK]
        stores[i].start()
    for store in stores:
        store.wait()


def pack_y(hz, cot):
    any_spec = pl.BlockSpec(memory_space=pl.ANY)
    piece = jax.ShapeDtypeStruct((256 + CY + 16, BLK), jnp.bfloat16)
    return pl.pallas_call(
        pack_y_kernel,
        out_shape=[piece, piece, piece],
        in_specs=[any_spec, any_spec],
        out_specs=[any_spec] * 3,
        scratch_shapes=[
            pltpu.VMEM((3, 128, CY), jnp.bfloat16),
            pltpu.VMEM((3, 256 + CY + 16, BLK), jnp.bfloat16),
            pltpu.SemaphoreType.DMA((9,)),
            pltpu.SemaphoreType.DMA((3,)),
        ],
        compiler_params=SMALL,
        cost_estimate=pl.CostEstimate(flops=0, bytes_accessed=3000000, transcendentals=0),
    )(hz, cot)


def spread(inverse, first_block, width):
    block = lax.broadcasted_iota(jnp.int32, (BLK, width), 0)
    column = lax.broadcasted_iota(jnp.int32, (BLK, width), 1)
    pick = jnp.where(block == first_block + column // BLK, 1.0, 0.0).astype(jnp.bfloat16)
    return jnp.dot(inverse, pick, preferred_element_type=jnp.float32)


def codes_y(lhs, part, i, scale):
    row = 256 + 256 * i
    both = jnp.concatenate([part[row : row + BLK], part[row + BLK : row + 2 * BLK]], axis=1)
    return round_clip(jnp.dot(lhs, both, preferred_element_type=jnp.float32) * scale)


def early_y_kernel(turned, hz, cot, q2, out, inverse, first, second, lhs, own, expo, sems):
    y, _ = place()
    start = HALF + CY * y
    loads = [
        pltpu.make_async_copy(hz.at[0, 0:256], lhs, sems.at[0]),
        pltpu.make_async_copy(hz.at[0, pl.ds(256 + CZ, 16)], expo, sems.at[1]),
        pltpu.make_async_copy(cot.at[:, pl.ds(pl.multiple_of(start, CY), CY)], own, sems.at[2]),
    ]
    for load in loads:
        load.start()
    count = turned.shape[0]
    exponent = jnp.concatenate([turned[...].astype(jnp.float32), jnp.zeros((BLK - count, 256), jnp.float32)], axis=0).T
    first[...] = exponent
    inverse[...] = power_two(-exponent).astype(jnp.bfloat16)
    for load in loads:
        load.wait()
    second[...] = expo[...].astype(jnp.float32)[0:8]
    for i in range(CY // 256):
        columns = slice(256 * i, 256 * i + 256)
        scale = spread(inverse[...], HALF // BLK + y * (CY // BLK) + 2 * i, 256)
        local = jnp.dot(lhs[...], own[:, columns], preferred_element_type=jnp.float32)
        total = round_clip(local * scale) + codes_y(q2[0:256], q2, i, scale)
        out[:, columns] = total.astype(jnp.bfloat16)


def early_y(turned, hz, cot, q2):
    any_spec = pl.BlockSpec(memory_space=pl.ANY)
    vmem_spec = pl.BlockSpec(memory_space=pltpu.VMEM)
    return pl.pallas_call(
        early_y_kernel,
        out_shape=[
            jax.ShapeDtypeStruct((256, CY), jnp.bfloat16),
            jax.ShapeDtypeStruct((256, BLK), jnp.bfloat16),
            jax.ShapeDtypeStruct((256, BLK), jnp.float32),
            jax.ShapeDtypeStruct((8, BLK), jnp.float32),
        ],
        in_specs=[vmem_spec, any_spec, any_spec, vmem_spec],
        out_specs=[vmem_spec] * 4,
        scratch_shapes=[
            pltpu.VMEM((256, BLK), jnp.bfloat16),
            pltpu.VMEM((128, CY), jnp.bfloat16),
            pltpu.VMEM((16, BLK), jnp.bfloat16),
            pltpu.SemaphoreType.DMA((3,)),
        ],
        compiler_params=SMALL,
        cost_estimate=pl.CostEstimate(flops=2 * 2 * 256 * 128 * CY, bytes_accessed=2000000, transcendentals=0),
    )(turned, hz, cot, *in_vmem(q2))


def late_y_kernel(inverse, first, second, early, q2, q1, q3, out, factor, diff, sums, sems):
    y, z = place()
    stores = []
    for i in range(CY // 256):
        columns = slice(256 * i, 256 * i + 256)
        scale = spread(inverse[...], HALF // BLK + y * (CY // BLK) + 2 * i, 256)
        total = early[:, columns].astype(jnp.float32)
        total = total + codes_y(q1[0:256], q1, i, scale) + codes_y(q3[0:256], q3, i, scale)
        for k in range(NZ):
            rows = [total[64 * j + 8 * Z_ORDER[k] : 64 * j + 8 * Z_ORDER[k] + 8] for j in range(NY)]
            sums[k, :, columns] = jnp.concatenate(rows, axis=0).astype(jnp.int16)
        stores.append(pltpu.make_async_copy(sums.at[:, :, columns], out.at[:, :, columns], sems.at[i]))
        stores[i].start()
    for step in range(NY):
        member = lax.rem(y + step, NY)
        expo = second[...]
        if step > 0:
            expo = (q3, q2, q1)[step - 1][256 + CY : 256 + CY + 16].astype(jnp.float32)[0:8]
        rows = pl.ds(pl.multiple_of(64 * member + 8 * z, 8), 8)
        diff[pl.ds(pl.multiple_of(8 * member, 8), 8)] = first[rows] - expo
    factor[...] = power_two(diff[...])
    for store in stores:
        store.wait()


def late_y(inverse, first, second, early, q2, q1, q3):
    vmem_spec = pl.BlockSpec(memory_space=pltpu.VMEM)
    shape = (NZ, 32, CY)
    return pl.pallas_call(
        late_y_kernel,
        out_shape=[pltpu.HBM(shape, jnp.int16), jax.ShapeDtypeStruct((32, BLK), jnp.float32)],
        in_specs=[vmem_spec] * 7,
        out_specs=[pl.BlockSpec(memory_space=pl.ANY), vmem_spec],
        scratch_shapes=[
            pltpu.VMEM((32, BLK), jnp.float32),
            pltpu.VMEM(shape, jnp.int16),
            pltpu.SemaphoreType.DMA((CY // 256,)),
        ],
        compiler_params=SMALL,
        cost_estimate=pl.CostEstimate(flops=2 * 2 * 256 * 128 * CY, bytes_accessed=2000000, transcendentals=0),
    )(inverse, first, second, *in_vmem(early, q2, q1, q3))


def sum_z_kernel(inverse, first, parts, own, s2, s1, s3, factor, total_ref, diff):
    y, z = place()
    for b in range(CZ // BLK):
        scale = spread(inverse[...], z * (CZ // BLK) + b, BLK)
        for h in range(2):
            total = jnp.zeros((BLK, BLK), jnp.float32)
            for r in range(NZ):
                local = jnp.dot(
                    parts[r, h * BLK : h * BLK + BLK],
                    parts[r, 256 + b * BLK : 256 + b * BLK + BLK],
                    preferred_element_type=jnp.float32,
                )
                total = total + round_clip(local * scale[h * BLK : h * BLK + BLK])
            total_ref[h * BLK : h * BLK + BLK, b * BLK : b * BLK + BLK] = total
    for step, out in zip((0,) + OFFS, (own, s2, s1, s3)):
        start = 64 * lax.rem(y + step + NY, NY)
        out[...] = total_ref[pl.ds(pl.multiple_of(start, 64), 64), :].astype(jnp.int16)
    for r in range(NZ):
        rows = pl.ds(pl.multiple_of(64 * y + 8 * Z_ORDER[r], 8), 8)
        expo = parts[r, 256 + CZ : 256 + CZ + 16].astype(jnp.float32)[0:8]
        diff[8 * Z_ORDER[r] : 8 * Z_ORDER[r] + 8] = first[rows] - expo
    factor[...] = power_two(diff[...])


def sum_z(inverse, first, parts):
    vmem_spec = pl.BlockSpec(memory_space=pltpu.VMEM)
    return pl.pallas_call(
        sum_z_kernel,
        out_shape=[pltpu.HBM((64, CZ), jnp.int16)]
        + [jax.ShapeDtypeStruct((64, CZ), jnp.int16)] * 3
        + [jax.ShapeDtypeStruct((64, BLK), jnp.float32)],
        in_specs=[vmem_spec] * 3,
        out_specs=[vmem_spec] * 5,
        scratch_shapes=[pltpu.VMEM((256, CZ), jnp.float32), pltpu.VMEM((64, BLK), jnp.float32)],
        compiler_params=SMALL,
        cost_estimate=pl.CostEstimate(flops=2 * 8 * 256 * 128 * CZ, bytes_accessed=3000000, transcendentals=0),
    )(inverse, first, *in_vmem(parts))


def second_kernel(factor_z, factor_y, own, s2, s1, s3, sy, out, own_here, sem):
    y, z = place()
    load = pltpu.make_async_copy(own, own_here, sem)
    load.start()
    scale = spread(factor_y[...].astype(jnp.bfloat16), HALF // BLK + y * (CY // BLK), CY)
    total = sy[0].astype(jnp.int32)
    for r in range(1, NZ):
        total = total + sy[r].astype(jnp.int32)
    codes = round_clip(total.astype(jnp.float32) * scale)
    for k in range(NY):
        for c in range(2):
            out[8 + 2 * k + c] = codes[8 * k : 8 * k + 8, c * CZ : c * CZ + CZ].astype(jnp.bfloat16)
    scale = spread(factor_z[...].astype(jnp.bfloat16), z * (CZ // BLK), CZ)
    total = s2[...].astype(jnp.int32) + s1[...].astype(jnp.int32) + s3[...].astype(jnp.int32)
    load.wait()
    total = total + own_here[...].astype(jnp.int32)
    codes = round_clip(total.astype(jnp.float32) * scale)
    for k in range(8):
        out[k] = codes[8 * k : 8 * k + 8].astype(jnp.bfloat16)


def second_codes(factor_z, factor_y, own, *arrays):
    vmem_spec = pl.BlockSpec(memory_space=pltpu.VMEM)
    return pl.pallas_call(
        second_kernel,
        out_shape=jax.ShapeDtypeStruct((NG, 8, CZ), jnp.bfloat16),
        in_specs=[vmem_spec, vmem_spec, pl.BlockSpec(memory_space=pl.ANY)] + [vmem_spec] * 4,
        out_specs=vmem_spec,
        scratch_shapes=[pltpu.VMEM((64, CZ), jnp.int16), pltpu.SemaphoreType.DMA],
        compiler_params=SMALL,
        cost_estimate=pl.CostEstimate(flops=4000000, bytes_accessed=2500000, transcendentals=0),
    )(*in_vmem(factor_z, factor_y), *in_hbm(own), *in_vmem(*arrays))


def body(acts, cotangent, first_exp, second_exp):
    group = lax.axis_index("inter")
    (far,) = in_hbm(cotangent)

    hz = pack_z(acts, second_exp, far)
    rz = lax.all_to_all(hz, "intra", 0, 0, axis_index_groups=Z_GROUPS, tiled=True)
    (near,) = in_hbm(hz)
    q2, q1, q3 = [lax.ppermute(p, "intra", y_shift(step)) for step, p in zip(OFFS, pack_y(near, far))]
    early, inverse, first, second = early_y(first_exp.T, near, far, q2)
    sy, factor_y = late_y(inverse, first, second, early, q2, q1, q3)
    ry = lax.all_to_all(sy, "intra", 0, 0, axis_index_groups=Z_GROUPS, tiled=True)
    own, s2, s1, s3, factor_z = sum_z(inverse, first, rz)
    t2, t1, t3 = [lax.ppermute(s, "intra", y_shift(step)) for step, s in zip(OFFS, (s2, s1, s3))]
    codes = second_codes(factor_z, factor_y, own, t2, t1, t3, ry)

    received = lax.all_to_all(codes, "inter", 0, 0, tiled=True)
    total = jnp.sum(received, axis=0, dtype=jnp.float32)
    rows = lax.ppermute(total, ("inter", "intra"), last_moves())
    my_exp = lax.dynamic_slice_in_dim(second_exp, group * (CZ // BLK), CZ // BLK, 1)
    return rows * (jnp.repeat(power_two(my_exp), BLK, axis=1) * (1.0 / (NG * NM)))


def solution(mesh):
    return jax.shard_map(
        body,
        mesh=mesh,
        in_specs=(P(("inter", "intra"), None), P(("inter", "intra"), None), P(), P("intra", None)),
        out_specs=P("intra", "inter"),
        check_vma=False,
    )
```

```python
import jax
import jax.numpy as jnp
from jax import lax
from jax.experimental import pallas as pl
from jax.experimental.pallas import tpu as pltpu
from jax.sharding import PartitionSpec as P

BLK = 128
NY = 4
NZ = 8
NG = 16
NM = NY * NZ
HALF = 7168
CZ = HALF // NZ
CY = HALF // NY
OFFS = (2, 1, -1)
MAGIC = 12582912.0
SMALL = pltpu.CompilerParams(vmem_limit_bytes=8 * 1024 * 1024)
FIRST_Z = 5
Z_ORDER = [(FIRST_Z + i) % NZ for i in range(NZ)]
Z_GROUPS = [[y * NZ + z for z in Z_ORDER] for y in range(NY)]


def y_shift(step):
    return [(y * NZ + z, ((y + step) % NY) * NZ + z) for y in range(NY) for z in range(NZ)]


def last_moves():
    moves = []
    for group in range(NG):
        for y in range(NY):
            for z in range(NZ):
                if group < 8:
                    target = z * NM + y * NZ + group
                else:
                    target = (8 + 2 * y + group % 2) * NM + ((group - 8) // 2) * NZ + z
                moves.append((group * NM + y * NZ + z, target))
    return moves


def power_two(expo):
    total = jnp.zeros(expo.shape, jnp.float32)
    for power in range(-8, 9):
        total = total + jnp.where(expo == power, jnp.float32(2.0**power), jnp.float32(0.0))
    return total


def in_vmem(*arrays):
    return [pltpu.with_memory_space_constraint(array, pltpu.VMEM) for array in arrays]


def in_hbm(*arrays):
    return [pltpu.with_memory_space_constraint(array, pltpu.HBM) for array in arrays]


def place():
    member = lax.axis_index("intra")
    return member // NZ, lax.rem(member, NZ)


def round_clip(values):
    return (jnp.clip(values, -127.0, 127.0) + MAGIC) - MAGIC


def pack_z_kernel(acts, exps, cot, out, wide, held, acts_here, exps_here, padded, into, outof):
    loads = [
        pltpu.make_async_copy(cot.at[:, z * CZ : (z + 1) * CZ], wide.at[j], into.at[j]) for j, z in enumerate(Z_ORDER)
    ]
    stores = [pltpu.make_async_copy(held.at[j], out.at[j], outof.at[j]) for j in range(NZ)]
    small = [
        pltpu.make_async_copy(acts, acts_here, into.at[NZ]),
        pltpu.make_async_copy(exps, exps_here, into.at[NZ + 1]),
    ]
    for load in small + loads:
        load.start()
    padded[...] = jnp.zeros((16, BLK), jnp.float32)
    for load in small:
        load.wait()
    turned = acts_here[...].T
    padded[0:8, 0 : exps.shape[1]] = exps_here[...].astype(jnp.float32)
    tail = padded[...].astype(jnp.bfloat16)
    for j in range(NZ):
        held[j, 0:256, :] = turned
        held[j, 256 + CZ : 256 + CZ + 16, :] = tail
        loads[j].wait()
        for b in range(CZ // BLK):
            held[j, 256 + b * BLK : 256 + b * BLK + BLK, :] = wide[j, :, b * BLK : b * BLK + BLK]
        stores[j].start()
    for store in stores:
        store.wait()


def pack_z(acts, exps, cot):
    shape = (NZ, 256 + CZ + 16, BLK)
    any_spec = pl.BlockSpec(memory_space=pl.ANY)
    return pl.pallas_call(
        pack_z_kernel,
        out_shape=jax.ShapeDtypeStruct(shape, jnp.bfloat16),
        in_specs=[any_spec, any_spec, any_spec],
        out_specs=any_spec,
        scratch_shapes=[
            pltpu.VMEM((NZ, 128, CZ), jnp.bfloat16),
            pltpu.VMEM(shape, jnp.bfloat16),
            pltpu.VMEM(acts.shape, jnp.bfloat16),
            pltpu.VMEM(exps.shape, jnp.int32),
            pltpu.VMEM((16, BLK), jnp.float32),
            pltpu.SemaphoreType.DMA((NZ + 2,)),
            pltpu.SemaphoreType.DMA((NZ,)),
        ],
        compiler_params=SMALL,
        cost_estimate=pl.CostEstimate(flops=0, bytes_accessed=4000000, transcendentals=0),
    )(*in_hbm(acts, exps, cot))


def pack_y_kernel(hz, cot, p2, p1, p3, wide, held, into, outof):
    y, _ = place()
    loads, stores = [], []
    for i, (step, out) in enumerate(zip(OFFS, (p2, p1, p3))):
        start = pl.multiple_of(HALF + CY * lax.rem(y + step + NY, NY), CY)
        moves = (
            (cot.at[:, pl.ds(start, CY)], wide.at[i]),
            (hz.at[0, 0:256], held.at[i, 0:256]),
            (hz.at[0, pl.ds(256 + CZ, 16)], held.at[i, pl.ds(256 + CY, 16)]),
        )
        loads += [pltpu.make_async_copy(src, dst, into.at[3 * i + k]) for k, (src, dst) in enumerate(moves)]
        stores.append(pltpu.make_async_copy(held.at[i], out, outof.at[i]))
    for load in loads:
        load.start()
    for i in range(3):
        for k in range(3):
            loads[3 * i + k].wait()
        for b in range(CY // BLK):
            held[i, 256 + b * BLK : 256 + b * BLK + BLK, :] = wide[i, :, b * BLK : b * BLK + BLK]
        stores[i].start()
    for store in stores:
        store.wait()


def pack_y(hz, cot):
    any_spec = pl.BlockSpec(memory_space=pl.ANY)
    piece = jax.ShapeDtypeStruct((256 + CY + 16, BLK), jnp.bfloat16)
    return pl.pallas_call(
        pack_y_kernel,
        out_shape=[piece, piece, piece],
        in_specs=[any_spec, any_spec],
        out_specs=[any_spec] * 3,
        scratch_shapes=[
            pltpu.VMEM((3, 128, CY), jnp.bfloat16),
            pltpu.VMEM((3, 256 + CY + 16, BLK), jnp.bfloat16),
            pltpu.SemaphoreType.DMA((9,)),
            pltpu.SemaphoreType.DMA((3,)),
        ],
        compiler_params=SMALL,
        cost_estimate=pl.CostEstimate(flops=0, bytes_accessed=3000000, transcendentals=0),
    )(hz, cot)


def spread(inverse, first_block, width):
    block = lax.broadcasted_iota(jnp.int32, (BLK, width), 0)
    column = lax.broadcasted_iota(jnp.int32, (BLK, width), 1)
    pick = jnp.where(block == first_block + column // BLK, 1.0, 0.0).astype(jnp.bfloat16)
    return jnp.dot(inverse, pick, preferred_element_type=jnp.float32)


def codes_y(lhs, part, i, scale):
    row = 256 + 256 * i
    both = jnp.concatenate([part[row : row + BLK], part[row + BLK : row + 2 * BLK]], axis=1)
    return round_clip(jnp.dot(lhs, both, preferred_element_type=jnp.float32) * scale)


def early_y_kernel(turned, hz, cot, q2, out, inverse, first, second, lhs, own, expo, sems):
    y, _ = place()
    start = HALF + CY * y
    loads = [
        pltpu.make_async_copy(hz.at[0, 0:256], lhs, sems.at[0]),
        pltpu.make_async_copy(hz.at[0, pl.ds(256 + CZ, 16)], expo, sems.at[1]),
        pltpu.make_async_copy(cot.at[:, pl.ds(pl.multiple_of(start, CY), CY)], own, sems.at[2]),
    ]
    for load in loads:
        load.start()
    count = turned.shape[0]
    exponent = jnp.concatenate([turned[...].astype(jnp.float32), jnp.zeros((BLK - count, 256), jnp.float32)], axis=0).T
    first[...] = exponent
    inverse[...] = power_two(-exponent).astype(jnp.bfloat16)
    for load in loads:
        load.wait()
    second[...] = expo[...].astype(jnp.float32)[0:8]
    for i in range(CY // 256):
        columns = slice(256 * i, 256 * i + 256)
        scale = spread(inverse[...], HALF // BLK + y * (CY // BLK) + 2 * i, 256)
        local = jnp.dot(lhs[...], own[:, columns], preferred_element_type=jnp.float32)
        total = round_clip(local * scale) + codes_y(q2[0:256], q2, i, scale)
        out[:, columns] = total.astype(jnp.bfloat16)


def early_y(turned, hz, cot, q2):
    any_spec = pl.BlockSpec(memory_space=pl.ANY)
    vmem_spec = pl.BlockSpec(memory_space=pltpu.VMEM)
    return pl.pallas_call(
        early_y_kernel,
        out_shape=[
            jax.ShapeDtypeStruct((256, CY), jnp.bfloat16),
            jax.ShapeDtypeStruct((256, BLK), jnp.bfloat16),
            jax.ShapeDtypeStruct((256, BLK), jnp.float32),
            jax.ShapeDtypeStruct((8, BLK), jnp.float32),
        ],
        in_specs=[vmem_spec, any_spec, any_spec, vmem_spec],
        out_specs=[vmem_spec] * 4,
        scratch_shapes=[
            pltpu.VMEM((256, BLK), jnp.bfloat16),
            pltpu.VMEM((128, CY), jnp.bfloat16),
            pltpu.VMEM((16, BLK), jnp.bfloat16),
            pltpu.SemaphoreType.DMA((3,)),
        ],
        compiler_params=SMALL,
        cost_estimate=pl.CostEstimate(flops=2 * 2 * 256 * 128 * CY, bytes_accessed=2000000, transcendentals=0),
    )(turned, hz, cot, *in_vmem(q2))


def late_y_kernel(inverse, first, second, early, q2, q1, q3, out, factor, diff, sums, sems):
    y, z = place()
    stores = []
    for i in range(CY // 256):
        columns = slice(256 * i, 256 * i + 256)
        scale = spread(inverse[...], HALF // BLK + y * (CY // BLK) + 2 * i, 256)
        total = early[:, columns].astype(jnp.float32)
        total = total + codes_y(q1[0:256], q1, i, scale) + codes_y(q3[0:256], q3, i, scale)
        for k in range(NZ):
            rows = [total[64 * j + 8 * Z_ORDER[k] : 64 * j + 8 * Z_ORDER[k] + 8] for j in range(NY)]
            sums[k, :, columns] = jnp.concatenate(rows, axis=0).astype(jnp.int16)
        stores.append(pltpu.make_async_copy(sums.at[:, :, columns], out.at[:, :, columns], sems.at[i]))
        stores[i].start()
    for step in range(NY):
        member = lax.rem(y + step, NY)
        expo = second[...]
        if step > 0:
            expo = (q3, q2, q1)[step - 1][256 + CY : 256 + CY + 16].astype(jnp.float32)[0:8]
        rows = pl.ds(pl.multiple_of(64 * member + 8 * z, 8), 8)
        diff[pl.ds(pl.multiple_of(8 * member, 8), 8)] = first[rows] - expo
    factor[...] = power_two(diff[...])
    for store in stores:
        store.wait()


def late_y(inverse, first, second, early, q2, q1, q3):
    vmem_spec = pl.BlockSpec(memory_space=pltpu.VMEM)
    shape = (NZ, 32, CY)
    return pl.pallas_call(
        late_y_kernel,
        out_shape=[pltpu.HBM(shape, jnp.int16), jax.ShapeDtypeStruct((32, BLK), jnp.float32)],
        in_specs=[vmem_spec] * 7,
        out_specs=[pl.BlockSpec(memory_space=pl.ANY), vmem_spec],
        scratch_shapes=[
            pltpu.VMEM((32, BLK), jnp.float32),
            pltpu.VMEM(shape, jnp.int16),
            pltpu.SemaphoreType.DMA((CY // 256,)),
        ],
        compiler_params=SMALL,
        cost_estimate=pl.CostEstimate(flops=2 * 2 * 256 * 128 * CY, bytes_accessed=2000000, transcendentals=0),
    )(inverse, first, second, *in_vmem(early, q2, q1, q3))


def sum_z_kernel(inverse, first, parts, own, s2, s1, s3, factor, total_ref, diff):
    y, z = place()
    for b in range(CZ // BLK):
        scale = spread(inverse[...], z * (CZ // BLK) + b, BLK)
        for h in range(2):
            total = jnp.zeros((BLK, BLK), jnp.float32)
            for r in range(NZ):
                local = jnp.dot(
                    parts[r, h * BLK : h * BLK + BLK],
                    parts[r, 256 + b * BLK : 256 + b * BLK + BLK],
                    preferred_element_type=jnp.float32,
                )
                total = total + round_clip(local * scale[h * BLK : h * BLK + BLK])
            total_ref[h * BLK : h * BLK + BLK, b * BLK : b * BLK + BLK] = total
    for step, out in zip((0,) + OFFS, (own, s2, s1, s3)):
        start = 64 * lax.rem(y + step + NY, NY)
        out[...] = total_ref[pl.ds(pl.multiple_of(start, 64), 64), :].astype(jnp.int16)
    for r in range(NZ):
        rows = pl.ds(pl.multiple_of(64 * y + 8 * Z_ORDER[r], 8), 8)
        expo = parts[r, 256 + CZ : 256 + CZ + 16].astype(jnp.float32)[0:8]
        diff[8 * Z_ORDER[r] : 8 * Z_ORDER[r] + 8] = first[rows] - expo
    factor[...] = power_two(diff[...])


def sum_z(inverse, first, parts):
    vmem_spec = pl.BlockSpec(memory_space=pltpu.VMEM)
    return pl.pallas_call(
        sum_z_kernel,
        out_shape=[pltpu.HBM((64, CZ), jnp.int16)]
        + [jax.ShapeDtypeStruct((64, CZ), jnp.int16)] * 3
        + [jax.ShapeDtypeStruct((64, BLK), jnp.float32)],
        in_specs=[vmem_spec] * 3,
        out_specs=[vmem_spec] * 5,
        scratch_shapes=[pltpu.VMEM((256, CZ), jnp.float32), pltpu.VMEM((64, BLK), jnp.float32)],
        compiler_params=SMALL,
        cost_estimate=pl.CostEstimate(flops=2 * 8 * 256 * 128 * CZ, bytes_accessed=3000000, transcendentals=0),
    )(inverse, first, *in_vmem(parts))


def second_z_kernel(factor, own, s2, s1, s3, out, own_here, codes_here, sems):
    _, z = place()
    load = pltpu.make_async_copy(own, own_here, sems.at[0])
    load.start()
    scale = spread(factor[...].astype(jnp.bfloat16), z * (CZ // BLK), CZ)
    total = s2[...].astype(jnp.int32) + s1[...].astype(jnp.int32) + s3[...].astype(jnp.int32)
    load.wait()
    total = total + own_here[...].astype(jnp.int32)
    codes = round_clip(total.astype(jnp.float32) * scale)
    for k in range(8):
        codes_here[k] = codes[8 * k : 8 * k + 8].astype(jnp.bfloat16)
    store = pltpu.make_async_copy(codes_here, out.at[0:8], sems.at[1])
    store.start()
    store.wait()


def second_z(factor, own, *arrays):
    any_spec = pl.BlockSpec(memory_space=pl.ANY)
    vmem_spec = pl.BlockSpec(memory_space=pltpu.VMEM)
    return pl.pallas_call(
        second_z_kernel,
        out_shape=pltpu.HBM((NG, 8, CZ), jnp.bfloat16),
        in_specs=[vmem_spec, any_spec] + [vmem_spec] * 3,
        out_specs=any_spec,
        scratch_shapes=[
            pltpu.VMEM((64, CZ), jnp.int16),
            pltpu.VMEM((8, 8, CZ), jnp.bfloat16),
            pltpu.SemaphoreType.DMA((2,)),
        ],
        compiler_params=SMALL,
        cost_estimate=pl.CostEstimate(flops=2000000, bytes_accessed=700000, transcendentals=0),
    )(*in_vmem(factor), *in_hbm(own), *in_vmem(*arrays))


def second_y_kernel(factor, sy, rest, out, codes_here, sem):
    y, _ = place()
    scale = spread(factor[...].astype(jnp.bfloat16), HALF // BLK + y * (CY // BLK), CY)
    total = sy[0].astype(jnp.int32)
    for r in range(1, NZ):
        total = total + sy[r].astype(jnp.int32)
    codes = round_clip(total.astype(jnp.float32) * scale)
    for k in range(NY):
        for c in range(2):
            codes_here[2 * k + c] = codes[8 * k : 8 * k + 8, c * CZ : c * CZ + CZ].astype(jnp.bfloat16)
    store = pltpu.make_async_copy(codes_here, out.at[8:16], sem)
    store.start()
    store.wait()


def second_y(factor, sy, rest):
    any_spec = pl.BlockSpec(memory_space=pl.ANY)
    vmem_spec = pl.BlockSpec(memory_space=pltpu.VMEM)
    return pl.pallas_call(
        second_y_kernel,
        out_shape=pltpu.HBM((NG, 8, CZ), jnp.bfloat16),
        in_specs=[vmem_spec, vmem_spec, any_spec],
        out_specs=any_spec,
        scratch_shapes=[pltpu.VMEM((8, 8, CZ), jnp.bfloat16), pltpu.SemaphoreType.DMA],
        input_output_aliases={2: 0},
        compiler_params=SMALL,
        cost_estimate=pl.CostEstimate(flops=2000000, bytes_accessed=1200000, transcendentals=0),
    )(*in_vmem(factor, sy), *in_hbm(rest))


def body(acts, cotangent, first_exp, second_exp):
    group = lax.axis_index("inter")
    (far,) = in_hbm(cotangent)

    hz = pack_z(acts, second_exp, far)
    rz = lax.all_to_all(hz, "intra", 0, 0, axis_index_groups=Z_GROUPS, tiled=True)
    (near,) = in_hbm(hz)
    q2, q1, q3 = [lax.ppermute(p, "intra", y_shift(step)) for step, p in zip(OFFS, pack_y(near, far))]
    early, inverse, first, second = early_y(first_exp.T, near, far, q2)
    sy, factor_y = late_y(inverse, first, second, early, q2, q1, q3)
    ry = lax.all_to_all(sy, "intra", 0, 0, axis_index_groups=Z_GROUPS, tiled=True)
    own, s2, s1, s3, factor_z = sum_z(inverse, first, rz)
    t2, t1, t3 = [lax.ppermute(s, "intra", y_shift(step)) for step, s in zip(OFFS, (s2, s1, s3))]
    codes = second_y(factor_y, ry, second_z(factor_z, own, t2, t1, t3))

    received = lax.all_to_all(codes, "inter", 0, 0, tiled=True)
    total = jnp.sum(received, axis=0, dtype=jnp.float32).astype(jnp.int16)
    rows = lax.ppermute(total, ("inter", "intra"), last_moves()).astype(jnp.float32)
    my_exp = lax.dynamic_slice_in_dim(second_exp, group * (CZ // BLK), CZ // BLK, 1)
    return rows * (jnp.repeat(power_two(my_exp), BLK, axis=1) * (1.0 / (NG * NM)))


def solution(mesh):
    return jax.shard_map(
        body,
        mesh=mesh,
        in_specs=(P(("inter", "intra"), None), P(("inter", "intra"), None), P(), P("intra", None)),
        out_specs=P("intra", "inter"),
        check_vma=False,
    )
```

```python
import jax
import jax.numpy as jnp
from jax import lax
from jax.experimental import pallas as pl
from jax.experimental.pallas import tpu as pltpu
from jax.sharding import PartitionSpec as P

BLK = 128
NY = 4
NZ = 8
NG = 16
NM = NY * NZ
HALF = 7168
CZ = HALF // NZ
CY = HALF // NY
OFFS = (2, 1, -1)
MAGIC = 12582912.0
SMALL = pltpu.CompilerParams(vmem_limit_bytes=8 * 1024 * 1024)
FIRST_Z = 5
Z_ORDER = [(FIRST_Z + i) % NZ for i in range(NZ)]
Z_GROUPS = [[y * NZ + z for z in Z_ORDER] for y in range(NY)]


def y_shift(step):
    return [(y * NZ + z, ((y + step) % NY) * NZ + z) for y in range(NY) for z in range(NZ)]


def last_moves():
    moves = []
    for group in range(NG):
        for y in range(NY):
            for z in range(NZ):
                if group < 8:
                    target = z * NM + y * NZ + group
                else:
                    target = (8 + 2 * y + group % 2) * NM + (((group - 8) // 2 + 2) % NY) * NZ + z
                moves.append((group * NM + y * NZ + z, target))
    return moves


def power_two(expo):
    total = jnp.zeros(expo.shape, jnp.float32)
    for power in range(-8, 9):
        total = total + jnp.where(expo == power, jnp.float32(2.0**power), jnp.float32(0.0))
    return total


def in_vmem(*arrays):
    return [pltpu.with_memory_space_constraint(array, pltpu.VMEM) for array in arrays]


def in_hbm(*arrays):
    return [pltpu.with_memory_space_constraint(array, pltpu.HBM) for array in arrays]


def place():
    member = lax.axis_index("intra")
    return member // NZ, lax.rem(member, NZ)


def round_clip(values):
    return (jnp.clip(values, -127.0, 127.0) + MAGIC) - MAGIC


def pack_z_kernel(acts, exps, cot, out, wide, held, acts_here, exps_here, padded, into, outof):
    loads = [
        pltpu.make_async_copy(cot.at[:, z * CZ : (z + 1) * CZ], wide.at[j], into.at[j]) for j, z in enumerate(Z_ORDER)
    ]
    stores = [pltpu.make_async_copy(held.at[j], out.at[j], outof.at[j]) for j in range(NZ)]
    small = [
        pltpu.make_async_copy(acts, acts_here, into.at[NZ]),
        pltpu.make_async_copy(exps, exps_here, into.at[NZ + 1]),
    ]
    for load in small + loads:
        load.start()
    padded[...] = jnp.zeros((16, BLK), jnp.float32)
    for load in small:
        load.wait()
    turned = acts_here[...].T
    padded[0:8, 0 : exps.shape[1]] = exps_here[...].astype(jnp.float32)
    tail = padded[...].astype(jnp.bfloat16)
    for j in range(NZ):
        held[j, 0:256, :] = turned
        held[j, 256 + CZ : 256 + CZ + 16, :] = tail
        loads[j].wait()
        for b in range(CZ // BLK):
            held[j, 256 + b * BLK : 256 + b * BLK + BLK, :] = wide[j, :, b * BLK : b * BLK + BLK]
        stores[j].start()
    for store in stores:
        store.wait()


def pack_z(acts, exps, cot):
    shape = (NZ, 256 + CZ + 16, BLK)
    any_spec = pl.BlockSpec(memory_space=pl.ANY)
    return pl.pallas_call(
        pack_z_kernel,
        out_shape=jax.ShapeDtypeStruct(shape, jnp.bfloat16),
        in_specs=[any_spec, any_spec, any_spec],
        out_specs=any_spec,
        scratch_shapes=[
            pltpu.VMEM((NZ, 128, CZ), jnp.bfloat16),
            pltpu.VMEM(shape, jnp.bfloat16),
            pltpu.VMEM(acts.shape, jnp.bfloat16),
            pltpu.VMEM(exps.shape, jnp.int32),
            pltpu.VMEM((16, BLK), jnp.float32),
            pltpu.SemaphoreType.DMA((NZ + 2,)),
            pltpu.SemaphoreType.DMA((NZ,)),
        ],
        compiler_params=SMALL,
        cost_estimate=pl.CostEstimate(flops=0, bytes_accessed=4000000, transcendentals=0),
    )(*in_hbm(acts, exps, cot))


def pack_y_kernel(hz, cot, p2, p1, p3, wide, held, into, outof):
    y, _ = place()
    loads, stores = [], []
    for i, (step, out) in enumerate(zip(OFFS, (p2, p1, p3))):
        start = pl.multiple_of(HALF + CY * lax.rem(y + step + NY, NY), CY)
        moves = (
            (cot.at[:, pl.ds(start, CY)], wide.at[i]),
            (hz.at[0, 0:256], held.at[i, 0:256]),
            (hz.at[0, pl.ds(256 + CZ, 16)], held.at[i, pl.ds(256 + CY, 16)]),
        )
        loads += [pltpu.make_async_copy(src, dst, into.at[3 * i + k]) for k, (src, dst) in enumerate(moves)]
        stores.append(pltpu.make_async_copy(held.at[i], out, outof.at[i]))
    for load in loads:
        load.start()
    for i in range(3):
        for k in range(3):
            loads[3 * i + k].wait()
        for b in range(CY // BLK):
            held[i, 256 + b * BLK : 256 + b * BLK + BLK, :] = wide[i, :, b * BLK : b * BLK + BLK]
        stores[i].start()
    for store in stores:
        store.wait()


def pack_y(hz, cot):
    any_spec = pl.BlockSpec(memory_space=pl.ANY)
    piece = jax.ShapeDtypeStruct((256 + CY + 16, BLK), jnp.bfloat16)
    return pl.pallas_call(
        pack_y_kernel,
        out_shape=[piece, piece, piece],
        in_specs=[any_spec, any_spec],
        out_specs=[any_spec] * 3,
        scratch_shapes=[
            pltpu.VMEM((3, 128, CY), jnp.bfloat16),
            pltpu.VMEM((3, 256 + CY + 16, BLK), jnp.bfloat16),
            pltpu.SemaphoreType.DMA((9,)),
            pltpu.SemaphoreType.DMA((3,)),
        ],
        compiler_params=SMALL,
        cost_estimate=pl.CostEstimate(flops=0, bytes_accessed=3000000, transcendentals=0),
    )(hz, cot)


def spread(inverse, first_block, width):
    block = lax.broadcasted_iota(jnp.int32, (BLK, width), 0)
    column = lax.broadcasted_iota(jnp.int32, (BLK, width), 1)
    pick = jnp.where(block == first_block + column // BLK, 1.0, 0.0).astype(jnp.bfloat16)
    return jnp.dot(inverse, pick, preferred_element_type=jnp.float32)


def codes_y(lhs, part, i, scale):
    row = 256 + 256 * i
    both = jnp.concatenate([part[row : row + BLK], part[row + BLK : row + 2 * BLK]], axis=1)
    return round_clip(jnp.dot(lhs, both, preferred_element_type=jnp.float32) * scale)


def early_y_kernel(turned, hz, cot, q2, out, inverse, first, second, lhs, own, expo, sems):
    y, _ = place()
    start = HALF + CY * y
    loads = [
        pltpu.make_async_copy(hz.at[0, 0:256], lhs, sems.at[0]),
        pltpu.make_async_copy(hz.at[0, pl.ds(256 + CZ, 16)], expo, sems.at[1]),
        pltpu.make_async_copy(cot.at[:, pl.ds(pl.multiple_of(start, CY), CY)], own, sems.at[2]),
    ]
    for load in loads:
        load.start()
    count = turned.shape[0]
    exponent = jnp.concatenate([turned[...].astype(jnp.float32), jnp.zeros((BLK - count, 256), jnp.float32)], axis=0).T
    first[...] = exponent
    inverse[...] = power_two(-exponent).astype(jnp.bfloat16)
    for load in loads:
        load.wait()
    second[...] = expo[...].astype(jnp.float32)[0:8]
    for i in range(CY // 256):
        columns = slice(256 * i, 256 * i + 256)
        scale = spread(inverse[...], HALF // BLK + y * (CY // BLK) + 2 * i, 256)
        local = jnp.dot(lhs[...], own[:, columns], preferred_element_type=jnp.float32)
        total = round_clip(local * scale) + codes_y(q2[0:256], q2, i, scale)
        out[:, columns] = total.astype(jnp.bfloat16)


def early_y(turned, hz, cot, q2):
    any_spec = pl.BlockSpec(memory_space=pl.ANY)
    vmem_spec = pl.BlockSpec(memory_space=pltpu.VMEM)
    return pl.pallas_call(
        early_y_kernel,
        out_shape=[
            jax.ShapeDtypeStruct((256, CY), jnp.bfloat16),
            jax.ShapeDtypeStruct((256, BLK), jnp.bfloat16),
            jax.ShapeDtypeStruct((256, BLK), jnp.float32),
            jax.ShapeDtypeStruct((8, BLK), jnp.float32),
        ],
        in_specs=[vmem_spec, any_spec, any_spec, vmem_spec],
        out_specs=[vmem_spec] * 4,
        scratch_shapes=[
            pltpu.VMEM((256, BLK), jnp.bfloat16),
            pltpu.VMEM((128, CY), jnp.bfloat16),
            pltpu.VMEM((16, BLK), jnp.bfloat16),
            pltpu.SemaphoreType.DMA((3,)),
        ],
        compiler_params=SMALL,
        cost_estimate=pl.CostEstimate(flops=2 * 2 * 256 * 128 * CY, bytes_accessed=2000000, transcendentals=0),
    )(turned, hz, cot, *in_vmem(q2))


def late_y_kernel(inverse, first, second, early, q2, q1, q3, out, factor, diff, sums, sems):
    y, z = place()
    stores = []
    for i in range(CY // 256):
        columns = slice(256 * i, 256 * i + 256)
        scale = spread(inverse[...], HALF // BLK + y * (CY // BLK) + 2 * i, 256)
        total = early[:, columns].astype(jnp.float32)
        total = total + codes_y(q1[0:256], q1, i, scale) + codes_y(q3[0:256], q3, i, scale)
        for k in range(NZ):
            rows = [total[64 * j + 8 * Z_ORDER[k] : 64 * j + 8 * Z_ORDER[k] + 8] for j in range(NY)]
            sums[k, :, columns] = jnp.concatenate(rows, axis=0).astype(jnp.int16)
        stores.append(pltpu.make_async_copy(sums.at[:, :, columns], out.at[:, :, columns], sems.at[i]))
        stores[i].start()
    for step in range(NY):
        member = lax.rem(y + step, NY)
        expo = second[...]
        if step > 0:
            expo = (q3, q2, q1)[step - 1][256 + CY : 256 + CY + 16].astype(jnp.float32)[0:8]
        rows = pl.ds(pl.multiple_of(64 * member + 8 * z, 8), 8)
        diff[pl.ds(pl.multiple_of(8 * member, 8), 8)] = first[rows] - expo
    factor[...] = power_two(diff[...])
    for store in stores:
        store.wait()


def late_y(inverse, first, second, early, q2, q1, q3):
    vmem_spec = pl.BlockSpec(memory_space=pltpu.VMEM)
    shape = (NZ, 32, CY)
    return pl.pallas_call(
        late_y_kernel,
        out_shape=[pltpu.HBM(shape, jnp.int16), jax.ShapeDtypeStruct((32, BLK), jnp.float32)],
        in_specs=[vmem_spec] * 7,
        out_specs=[pl.BlockSpec(memory_space=pl.ANY), vmem_spec],
        scratch_shapes=[
            pltpu.VMEM((32, BLK), jnp.float32),
            pltpu.VMEM(shape, jnp.int16),
            pltpu.SemaphoreType.DMA((CY // 256,)),
        ],
        compiler_params=SMALL,
        cost_estimate=pl.CostEstimate(flops=2 * 2 * 256 * 128 * CY, bytes_accessed=2000000, transcendentals=0),
    )(inverse, first, second, *in_vmem(early, q2, q1, q3))


def sum_z_kernel(inverse, first, parts, own, s2, s1, s3, factor, total_ref, diff):
    y, z = place()
    for b in range(CZ // BLK):
        scale = spread(inverse[...], z * (CZ // BLK) + b, BLK)
        for h in range(2):
            total = jnp.zeros((BLK, BLK), jnp.float32)
            for r in range(NZ):
                local = jnp.dot(
                    parts[r, h * BLK : h * BLK + BLK],
                    parts[r, 256 + b * BLK : 256 + b * BLK + BLK],
                    preferred_element_type=jnp.float32,
                )
                total = total + round_clip(local * scale[h * BLK : h * BLK + BLK])
            total_ref[h * BLK : h * BLK + BLK, b * BLK : b * BLK + BLK] = total
    for step, out in zip((0,) + OFFS, (own, s2, s1, s3)):
        start = 64 * lax.rem(y + step + NY, NY)
        out[...] = total_ref[pl.ds(pl.multiple_of(start, 64), 64), :].astype(jnp.int16)
    for r in range(NZ):
        rows = pl.ds(pl.multiple_of(64 * y + 8 * Z_ORDER[r], 8), 8)
        expo = parts[r, 256 + CZ : 256 + CZ + 16].astype(jnp.float32)[0:8]
        diff[8 * Z_ORDER[r] : 8 * Z_ORDER[r] + 8] = first[rows] - expo
    factor[...] = power_two(diff[...])


def sum_z(inverse, first, parts):
    vmem_spec = pl.BlockSpec(memory_space=pltpu.VMEM)
    return pl.pallas_call(
        sum_z_kernel,
        out_shape=[pltpu.HBM((64, CZ), jnp.int16)]
        + [jax.ShapeDtypeStruct((64, CZ), jnp.int16)] * 3
        + [jax.ShapeDtypeStruct((64, BLK), jnp.float32)],
        in_specs=[vmem_spec] * 3,
        out_specs=[vmem_spec] * 5,
        scratch_shapes=[pltpu.VMEM((256, CZ), jnp.float32), pltpu.VMEM((64, BLK), jnp.float32)],
        compiler_params=SMALL,
        cost_estimate=pl.CostEstimate(flops=2 * 8 * 256 * 128 * CZ, bytes_accessed=3000000, transcendentals=0),
    )(inverse, first, *in_vmem(parts))


def second_z_kernel(factor, own, s2, s1, s3, out, own_here, sem):
    _, z = place()
    load = pltpu.make_async_copy(own, own_here, sem)
    load.start()
    scale = spread(factor[...].astype(jnp.bfloat16), z * (CZ // BLK), CZ)
    total = s2[...].astype(jnp.int32) + s1[...].astype(jnp.int32) + s3[...].astype(jnp.int32)
    load.wait()
    total = total + own_here[...].astype(jnp.int32)
    codes = round_clip(total.astype(jnp.float32) * scale)
    for k in range(8):
        out[k] = codes[8 * k : 8 * k + 8].astype(jnp.bfloat16)


def second_z(factor, own, *arrays):
    vmem_spec = pl.BlockSpec(memory_space=pltpu.VMEM)
    return pl.pallas_call(
        second_z_kernel,
        out_shape=jax.ShapeDtypeStruct((8, 8, CZ), jnp.bfloat16),
        in_specs=[vmem_spec, pl.BlockSpec(memory_space=pl.ANY)] + [vmem_spec] * 3,
        out_specs=vmem_spec,
        scratch_shapes=[pltpu.VMEM((64, CZ), jnp.int16), pltpu.SemaphoreType.DMA],
        compiler_params=SMALL,
        cost_estimate=pl.CostEstimate(flops=2000000, bytes_accessed=700000, transcendentals=0),
    )(*in_vmem(factor), *in_hbm(own), *in_vmem(*arrays))


def second_y_kernel(factor, sy, rest, out, codes_here, sems):
    y, _ = place()
    first_half = pltpu.make_async_copy(rest, out.at[0:8], sems.at[0])
    first_half.start()
    scale = spread(factor[...].astype(jnp.bfloat16), HALF // BLK + y * (CY // BLK), CY)
    total = sy[0].astype(jnp.int32)
    for r in range(1, NZ):
        total = total + sy[r].astype(jnp.int32)
    codes = round_clip(total.astype(jnp.float32) * scale)
    for k in range(NY):
        for c in range(2):
            codes_here[(2 * k + 4) % 8 + c] = codes[8 * k : 8 * k + 8, c * CZ : c * CZ + CZ].astype(jnp.bfloat16)
    second_half = pltpu.make_async_copy(codes_here, out.at[8:16], sems.at[1])
    second_half.start()
    first_half.wait()
    second_half.wait()


def second_y(factor, sy, rest):
    any_spec = pl.BlockSpec(memory_space=pl.ANY)
    vmem_spec = pl.BlockSpec(memory_space=pltpu.VMEM)
    return pl.pallas_call(
        second_y_kernel,
        out_shape=pltpu.HBM((NG, 8, CZ), jnp.bfloat16),
        in_specs=[vmem_spec] * 3,
        out_specs=any_spec,
        scratch_shapes=[pltpu.VMEM((8, 8, CZ), jnp.bfloat16), pltpu.SemaphoreType.DMA((2,))],
        compiler_params=SMALL,
        cost_estimate=pl.CostEstimate(flops=2000000, bytes_accessed=1200000, transcendentals=0),
    )(*in_vmem(factor, sy, rest))


def body(acts, cotangent, first_exp, second_exp):
    group = lax.axis_index("inter")
    (far,) = in_hbm(cotangent)

    hz = pack_z(acts, second_exp, far)
    rz = lax.all_to_all(hz, "intra", 0, 0, axis_index_groups=Z_GROUPS, tiled=True)
    (near,) = in_hbm(hz)
    q2, q1, q3 = [lax.ppermute(p, "intra", y_shift(step)) for step, p in zip(OFFS, pack_y(near, far))]
    early, inverse, first, second = early_y(first_exp.T, near, far, q2)
    sy, factor_y = late_y(inverse, first, second, early, q2, q1, q3)
    ry = lax.all_to_all(sy, "intra", 0, 0, axis_index_groups=Z_GROUPS, tiled=True)
    own, s2, s1, s3, factor_z = sum_z(inverse, first, rz)
    t2, t1, t3 = [lax.ppermute(s, "intra", y_shift(step)) for step, s in zip(OFFS, (s2, s1, s3))]
    codes = second_y(factor_y, ry, second_z(factor_z, own, t2, t1, t3))

    received = lax.all_to_all(codes, "inter", 0, 0, tiled=True)
    total = jnp.sum(received, axis=0, dtype=jnp.float32).astype(jnp.int16)
    rows = lax.ppermute(total, ("inter", "intra"), last_moves()).astype(jnp.float32)
    my_exp = lax.dynamic_slice_in_dim(second_exp, group * (CZ // BLK), CZ // BLK, 1)
    return rows * (jnp.repeat(power_two(my_exp), BLK, axis=1) * (1.0 / (NG * NM)))


def solution(mesh):
    return jax.shard_map(
        body,
        mesh=mesh,
        in_specs=(P(("inter", "intra"), None), P(("inter", "intra"), None), P(), P("intra", None)),
        out_specs=P("intra", "inter"),
        check_vma=False,
    )
```

```python
import jax
import jax.numpy as jnp
from jax import lax
from jax.experimental import pallas as pl
from jax.experimental.pallas import tpu as pltpu
from jax.sharding import PartitionSpec as P

BLK = 128
NY = 4
NZ = 8
NG = 16
NM = NY * NZ
HALF = 7168
CZ = HALF // NZ
CY = HALF // NY
OFFS = (2, 1, -1)
MAGIC = 12582912.0
SMALL = pltpu.CompilerParams(vmem_limit_bytes=8 * 1024 * 1024)
FIRST_Z = 5
Z_ORDER = [(FIRST_Z + i) % NZ for i in range(NZ)]
Z_OWNER = [0, 1, 2, 7, 4, 5, 6, 3]
Z_GROUPS = [[y * NZ + z for z in Z_ORDER] for y in range(NY)]


def y_shift(step):
    return [(y * NZ + z, ((y + step) % NY) * NZ + z) for y in range(NY) for z in range(NZ)]


def last_moves():
    moves = []
    for group in range(NG):
        for y in range(NY):
            for z in range(NZ):
                if group < 8:
                    target = Z_OWNER[z] * NM + y * NZ + (group + 4) % 8
                else:
                    target = (8 + 2 * y + group % 2) * NM + (((group - 8) // 2 + 2) % NY) * NZ + z
                moves.append((group * NM + y * NZ + z, target))
    return moves


def power_two(expo):
    total = jnp.zeros(expo.shape, jnp.float32)
    for power in range(-8, 9):
        total = total + jnp.where(expo == power, jnp.float32(2.0**power), jnp.float32(0.0))
    return total


def in_vmem(*arrays):
    return [pltpu.with_memory_space_constraint(array, pltpu.VMEM) for array in arrays]


def in_hbm(*arrays):
    return [pltpu.with_memory_space_constraint(array, pltpu.HBM) for array in arrays]


def place():
    member = lax.axis_index("intra")
    return member // NZ, lax.rem(member, NZ)


def owner_of(z):
    return jnp.where((z == 3) | (z == 7), 10 - z, z)


def round_clip(values):
    return (jnp.clip(values, -127.0, 127.0) + MAGIC) - MAGIC


def pack_z_kernel(acts, exps, cot, out, wide, held, acts_here, exps_here, padded, into, outof):
    loads = [
        pltpu.make_async_copy(cot.at[:, c * CZ : (c + 1) * CZ], wide.at[j], into.at[j])
        for j, c in enumerate(Z_OWNER[z] for z in Z_ORDER)
    ]
    stores = [pltpu.make_async_copy(held.at[j], out.at[j], outof.at[j]) for j in range(NZ)]
    small = [
        pltpu.make_async_copy(acts, acts_here, into.at[NZ]),
        pltpu.make_async_copy(exps, exps_here, into.at[NZ + 1]),
    ]
    for load in small + loads:
        load.start()
    padded[...] = jnp.zeros((16, BLK), jnp.float32)
    for load in small:
        load.wait()
    turned = acts_here[...].T
    padded[0:8, 0 : exps.shape[1]] = exps_here[...].astype(jnp.float32)
    tail = padded[...].astype(jnp.bfloat16)
    for j in range(NZ):
        held[j, 0:256, :] = turned
        held[j, 256 + CZ : 256 + CZ + 16, :] = tail
        loads[j].wait()
        for b in range(CZ // BLK):
            held[j, 256 + b * BLK : 256 + b * BLK + BLK, :] = wide[j, :, b * BLK : b * BLK + BLK]
        stores[j].start()
    for store in stores:
        store.wait()


def pack_z(acts, exps, cot):
    shape = (NZ, 256 + CZ + 16, BLK)
    any_spec = pl.BlockSpec(memory_space=pl.ANY)
    return pl.pallas_call(
        pack_z_kernel,
        out_shape=jax.ShapeDtypeStruct(shape, jnp.bfloat16),
        in_specs=[any_spec, any_spec, any_spec],
        out_specs=any_spec,
        scratch_shapes=[
            pltpu.VMEM((NZ, 128, CZ), jnp.bfloat16),
            pltpu.VMEM(shape, jnp.bfloat16),
            pltpu.VMEM(acts.shape, jnp.bfloat16),
            pltpu.VMEM(exps.shape, jnp.int32),
            pltpu.VMEM((16, BLK), jnp.float32),
            pltpu.SemaphoreType.DMA((NZ + 2,)),
            pltpu.SemaphoreType.DMA((NZ,)),
        ],
        compiler_params=SMALL,
        cost_estimate=pl.CostEstimate(flops=0, bytes_accessed=4000000, transcendentals=0),
    )(*in_hbm(acts, exps, cot))


def pack_y_kernel(hz, cot, p2, p1, p3, wide, held, into, outof):
    y, _ = place()
    loads, stores = [], []
    for i, (step, out) in enumerate(zip(OFFS, (p2, p1, p3))):
        start = pl.multiple_of(HALF + CY * lax.rem(y + step + NY, NY), CY)
        moves = (
            (cot.at[:, pl.ds(start, CY)], wide.at[i]),
            (hz.at[0, 0:256], held.at[i, 0:256]),
            (hz.at[0, pl.ds(256 + CZ, 16)], held.at[i, pl.ds(256 + CY, 16)]),
        )
        loads += [pltpu.make_async_copy(src, dst, into.at[3 * i + k]) for k, (src, dst) in enumerate(moves)]
        stores.append(pltpu.make_async_copy(held.at[i], out, outof.at[i]))
    for load in loads:
        load.start()
    for i in range(3):
        for k in range(3):
            loads[3 * i + k].wait()
        for b in range(CY // BLK):
            held[i, 256 + b * BLK : 256 + b * BLK + BLK, :] = wide[i, :, b * BLK : b * BLK + BLK]
        stores[i].start()
    for store in stores:
        store.wait()


def pack_y(hz, cot):
    any_spec = pl.BlockSpec(memory_space=pl.ANY)
    piece = jax.ShapeDtypeStruct((256 + CY + 16, BLK), jnp.bfloat16)
    return pl.pallas_call(
        pack_y_kernel,
        out_shape=[piece, piece, piece],
        in_specs=[any_spec, any_spec],
        out_specs=[any_spec] * 3,
        scratch_shapes=[
            pltpu.VMEM((3, 128, CY), jnp.bfloat16),
            pltpu.VMEM((3, 256 + CY + 16, BLK), jnp.bfloat16),
            pltpu.SemaphoreType.DMA((9,)),
            pltpu.SemaphoreType.DMA((3,)),
        ],
        compiler_params=SMALL,
        cost_estimate=pl.CostEstimate(flops=0, bytes_accessed=3000000, transcendentals=0),
    )(hz, cot)


def spread(inverse, first_block, width):
    block = lax.broadcasted_iota(jnp.int32, (BLK, width), 0)
    column = lax.broadcasted_iota(jnp.int32, (BLK, width), 1)
    pick = jnp.where(block == first_block + column // BLK, 1.0, 0.0).astype(jnp.bfloat16)
    return jnp.dot(inverse, pick, preferred_element_type=jnp.float32)


def codes_y(lhs, part, i, scale):
    row = 256 + 256 * i
    both = jnp.concatenate([part[row : row + BLK], part[row + BLK : row + 2 * BLK]], axis=1)
    return round_clip(jnp.dot(lhs, both, preferred_element_type=jnp.float32) * scale)


def early_y_kernel(turned, hz, cot, q2, out, inverse, first, second, lhs, own, expo, sems):
    y, _ = place()
    start = HALF + CY * y
    loads = [
        pltpu.make_async_copy(hz.at[0, 0:256], lhs, sems.at[0]),
        pltpu.make_async_copy(hz.at[0, pl.ds(256 + CZ, 16)], expo, sems.at[1]),
        pltpu.make_async_copy(cot.at[:, pl.ds(pl.multiple_of(start, CY), CY)], own, sems.at[2]),
    ]
    for load in loads:
        load.start()
    count = turned.shape[0]
    exponent = jnp.concatenate([turned[...].astype(jnp.float32), jnp.zeros((BLK - count, 256), jnp.float32)], axis=0).T
    first[...] = exponent
    inverse[...] = power_two(-exponent).astype(jnp.bfloat16)
    for load in loads:
        load.wait()
    second[...] = expo[...].astype(jnp.float32)[0:8]
    for i in range(CY // 256):
        columns = slice(256 * i, 256 * i + 256)
        scale = spread(inverse[...], HALF // BLK + y * (CY // BLK) + 2 * i, 256)
        local = jnp.dot(lhs[...], own[:, columns], preferred_element_type=jnp.float32)
        total = round_clip(local * scale) + codes_y(q2[0:256], q2, i, scale)
        out[:, columns] = total.astype(jnp.bfloat16)


def early_y(turned, hz, cot, q2):
    any_spec = pl.BlockSpec(memory_space=pl.ANY)
    vmem_spec = pl.BlockSpec(memory_space=pltpu.VMEM)
    return pl.pallas_call(
        early_y_kernel,
        out_shape=[
            jax.ShapeDtypeStruct((256, CY), jnp.bfloat16),
            jax.ShapeDtypeStruct((256, BLK), jnp.bfloat16),
            jax.ShapeDtypeStruct((256, BLK), jnp.float32),
            jax.ShapeDtypeStruct((8, BLK), jnp.float32),
        ],
        in_specs=[vmem_spec, any_spec, any_spec, vmem_spec],
        out_specs=[vmem_spec] * 4,
        scratch_shapes=[
            pltpu.VMEM((256, BLK), jnp.bfloat16),
            pltpu.VMEM((128, CY), jnp.bfloat16),
            pltpu.VMEM((16, BLK), jnp.bfloat16),
            pltpu.SemaphoreType.DMA((3,)),
        ],
        compiler_params=SMALL,
        cost_estimate=pl.CostEstimate(flops=2 * 2 * 256 * 128 * CY, bytes_accessed=2000000, transcendentals=0),
    )(turned, hz, cot, *in_vmem(q2))


def late_y_kernel(inverse, first, second, early, q2, q1, q3, out, factor, diff, sums, sems):
    y, z = place()
    stores = []
    for i in range(CY // 256):
        columns = slice(256 * i, 256 * i + 256)
        scale = spread(inverse[...], HALF // BLK + y * (CY // BLK) + 2 * i, 256)
        total = early[:, columns].astype(jnp.float32)
        total = total + codes_y(q1[0:256], q1, i, scale) + codes_y(q3[0:256], q3, i, scale)
        for k in range(NZ):
            rows = [total[64 * j + 8 * Z_ORDER[k] : 64 * j + 8 * Z_ORDER[k] + 8] for j in range(NY)]
            sums[k, :, columns] = jnp.concatenate(rows, axis=0).astype(jnp.int16)
        stores.append(pltpu.make_async_copy(sums.at[:, :, columns], out.at[:, :, columns], sems.at[i]))
        stores[i].start()
    for step in range(NY):
        member = lax.rem(y + step, NY)
        expo = second[...]
        if step > 0:
            expo = (q3, q2, q1)[step - 1][256 + CY : 256 + CY + 16].astype(jnp.float32)[0:8]
        rows = pl.ds(pl.multiple_of(64 * member + 8 * z, 8), 8)
        diff[pl.ds(pl.multiple_of(8 * member, 8), 8)] = first[rows] - expo
    factor[...] = power_two(diff[...])
    for store in stores:
        store.wait()


def late_y(inverse, first, second, early, q2, q1, q3):
    vmem_spec = pl.BlockSpec(memory_space=pltpu.VMEM)
    shape = (NZ, 32, CY)
    return pl.pallas_call(
        late_y_kernel,
        out_shape=[pltpu.HBM(shape, jnp.int16), jax.ShapeDtypeStruct((32, BLK), jnp.float32)],
        in_specs=[vmem_spec] * 7,
        out_specs=[pl.BlockSpec(memory_space=pl.ANY), vmem_spec],
        scratch_shapes=[
            pltpu.VMEM((32, BLK), jnp.float32),
            pltpu.VMEM(shape, jnp.int16),
            pltpu.SemaphoreType.DMA((CY // 256,)),
        ],
        compiler_params=SMALL,
        cost_estimate=pl.CostEstimate(flops=2 * 2 * 256 * 128 * CY, bytes_accessed=2000000, transcendentals=0),
    )(inverse, first, second, *in_vmem(early, q2, q1, q3))


def sum_z_kernel(inverse, first, parts, own, s2, s1, s3, factor, total_ref, diff):
    y, z = place()
    for b in range(CZ // BLK):
        scale = spread(inverse[...], owner_of(z) * (CZ // BLK) + b, BLK)
        for h in range(2):
            total = jnp.zeros((BLK, BLK), jnp.float32)
            for r in range(NZ):
                local = jnp.dot(
                    parts[r, h * BLK : h * BLK + BLK],
                    parts[r, 256 + b * BLK : 256 + b * BLK + BLK],
                    preferred_element_type=jnp.float32,
                )
                total = total + round_clip(local * scale[h * BLK : h * BLK + BLK])
            total_ref[h * BLK : h * BLK + BLK, b * BLK : b * BLK + BLK] = total
    for step, out in zip((0,) + OFFS, (own, s2, s1, s3)):
        start = 64 * lax.rem(y + step + NY, NY)
        out[...] = total_ref[pl.ds(pl.multiple_of(start, 64), 64), :].astype(jnp.int16)
    for r in range(NZ):
        rows = pl.ds(pl.multiple_of(64 * y + 8 * Z_ORDER[r], 8), 8)
        expo = parts[r, 256 + CZ : 256 + CZ + 16].astype(jnp.float32)[0:8]
        diff[8 * Z_ORDER[r] : 8 * Z_ORDER[r] + 8] = first[rows] - expo
    factor[...] = power_two(diff[...])


def sum_z(inverse, first, parts):
    vmem_spec = pl.BlockSpec(memory_space=pltpu.VMEM)
    return pl.pallas_call(
        sum_z_kernel,
        out_shape=[pltpu.HBM((64, CZ), jnp.int16)]
        + [jax.ShapeDtypeStruct((64, CZ), jnp.int16)] * 3
        + [jax.ShapeDtypeStruct((64, BLK), jnp.float32)],
        in_specs=[vmem_spec] * 3,
        out_specs=[vmem_spec] * 5,
        scratch_shapes=[pltpu.VMEM((256, CZ), jnp.float32), pltpu.VMEM((64, BLK), jnp.float32)],
        compiler_params=SMALL,
        cost_estimate=pl.CostEstimate(flops=2 * 8 * 256 * 128 * CZ, bytes_accessed=3000000, transcendentals=0),
    )(inverse, first, *in_vmem(parts))


def second_z_kernel(factor, own, s2, s1, s3, out, own_here, sem):
    _, z = place()
    load = pltpu.make_async_copy(own, own_here, sem)
    load.start()
    scale = spread(factor[...].astype(jnp.bfloat16), owner_of(z) * (CZ // BLK), CZ)
    total = s2[...].astype(jnp.int32) + s1[...].astype(jnp.int32) + s3[...].astype(jnp.int32)
    load.wait()
    total = total + own_here[...].astype(jnp.int32)
    codes = round_clip(total.astype(jnp.float32) * scale)
    for k in range(8):
        out[(k + 4) % 8] = codes[8 * k : 8 * k + 8].astype(jnp.bfloat16)


def second_z(factor, own, *arrays):
    vmem_spec = pl.BlockSpec(memory_space=pltpu.VMEM)
    return pl.pallas_call(
        second_z_kernel,
        out_shape=jax.ShapeDtypeStruct((8, 8, CZ), jnp.bfloat16),
        in_specs=[vmem_spec, pl.BlockSpec(memory_space=pl.ANY)] + [vmem_spec] * 3,
        out_specs=vmem_spec,
        scratch_shapes=[pltpu.VMEM((64, CZ), jnp.int16), pltpu.SemaphoreType.DMA],
        compiler_params=SMALL,
        cost_estimate=pl.CostEstimate(flops=2000000, bytes_accessed=700000, transcendentals=0),
    )(*in_vmem(factor), *in_hbm(own), *in_vmem(*arrays))


def second_y_kernel(factor, sy, rest, out, codes_here, sems):
    y, _ = place()
    first_half = pltpu.make_async_copy(rest, out.at[0:8], sems.at[0])
    first_half.start()
    scale = spread(factor[...].astype(jnp.bfloat16), HALF // BLK + y * (CY // BLK), CY)
    total = sy[0].astype(jnp.int32)
    for r in range(1, NZ):
        total = total + sy[r].astype(jnp.int32)
    codes = round_clip(total.astype(jnp.float32) * scale)
    for k in range(NY):
        for c in range(2):
            codes_here[(2 * k + 4) % 8 + c] = codes[8 * k : 8 * k + 8, c * CZ : c * CZ + CZ].astype(jnp.bfloat16)
    second_half = pltpu.make_async_copy(codes_here, out.at[8:16], sems.at[1])
    second_half.start()
    first_half.wait()
    second_half.wait()


def second_y(factor, sy, rest):
    any_spec = pl.BlockSpec(memory_space=pl.ANY)
    vmem_spec = pl.BlockSpec(memory_space=pltpu.VMEM)
    return pl.pallas_call(
        second_y_kernel,
        out_shape=pltpu.HBM((NG, 8, CZ), jnp.bfloat16),
        in_specs=[vmem_spec] * 3,
        out_specs=any_spec,
        scratch_shapes=[pltpu.VMEM((8, 8, CZ), jnp.bfloat16), pltpu.SemaphoreType.DMA((2,))],
        compiler_params=SMALL,
        cost_estimate=pl.CostEstimate(flops=2000000, bytes_accessed=1200000, transcendentals=0),
    )(*in_vmem(factor, sy, rest))


def body(acts, cotangent, first_exp, second_exp):
    group = lax.axis_index("inter")
    (far,) = in_hbm(cotangent)

    hz = pack_z(acts, second_exp, far)
    rz = lax.all_to_all(hz, "intra", 0, 0, axis_index_groups=Z_GROUPS, tiled=True)
    (near,) = in_hbm(hz)
    q2, q1, q3 = [lax.ppermute(p, "intra", y_shift(step)) for step, p in zip(OFFS, pack_y(near, far))]
    early, inverse, first, second = early_y(first_exp.T, near, far, q2)
    sy, factor_y = late_y(inverse, first, second, early, q2, q1, q3)
    ry = lax.all_to_all(sy, "intra", 0, 0, axis_index_groups=Z_GROUPS, tiled=True)
    own, s2, s1, s3, factor_z = sum_z(inverse, first, rz)
    t2, t1, t3 = [lax.ppermute(s, "intra", y_shift(step)) for step, s in zip(OFFS, (s2, s1, s3))]
    codes = second_y(factor_y, ry, second_z(factor_z, own, t2, t1, t3))

    received = lax.all_to_all(codes, "inter", 0, 0, tiled=True)
    total = jnp.sum(received, axis=0, dtype=jnp.float32).astype(jnp.int16)
    rows = lax.ppermute(total, ("inter", "intra"), last_moves()).astype(jnp.float32)
    my_exp = lax.dynamic_slice_in_dim(second_exp, group * (CZ // BLK), CZ // BLK, 1)
    return rows * (jnp.repeat(power_two(my_exp), BLK, axis=1) * (1.0 / (NG * NM)))


def solution(mesh):
    return jax.shard_map(
        body,
        mesh=mesh,
        in_specs=(P(("inter", "intra"), None), P(("inter", "intra"), None), P(), P("intra", None)),
        out_specs=P("intra", "inter"),
        check_vma=False,
    )
```
